256 devices in a mesh: dp: 2 (over z_lo), row: 8 (over x, core), col: 16 (over y, z_hi).
Axes of the slice: x: 4, y: 4, z: 8 (z_hi: 4, z_lo: 2; z = z_hi * 2 + z_lo), core: 2. Of those that a mesh axis runs over, the one named last changes fastest.
Arguments:
- hidden_input: bfloat16 [512, 16384], P('dp', ('row', 'col')), may hold values from -10 to 10
- doc_ids: int32 [2, 256], P('dp'), may hold values from 0 to 7, never falling along the last dimension, each value on 1 to 128 neighbouring positions
- cotangent: bfloat16 [512, 16384], P('dp', ('row', 'col')), may hold values from -6 to 6
- query_matrix: bfloat16 [16384, 16384], P('row', 'col'), may hold values from -0.046875 to 0.046875
- key_matrix: bfloat16 [16384, 1024], P('row', 'col'), may hold values from -0.046875 to 0.046875
- value_matrix: bfloat16 [16384, 1024], P('row', 'col'), may hold values from -0.046875 to 0.046875
- output_matrix: bfloat16 [16384, 16384], P('col', 'row'), may hold values from -0.046875 to 0.046875
- query_down: bfloat16 [64, 16384], P(None, 'row'), may hold values from -0.046875 to 0.046875
- query_raise_map: bfloat16 [64, 16384], P(None, 'col'), may hold values from -0.75 to 0.75
- key_down: bfloat16 [64, 16384], P(None, 'row'), may hold values from -0.046875 to 0.046875
- key_raise_map: bfloat16 [64, 1024], P(None, 'col'), may hold values from -0.75 to 0.75
- value_down: bfloat16 [64, 16384], P(None, 'row'), may hold values from -0.046875 to 0.046875
- value_raise_map: bfloat16 [64, 1024], P(None, 'col'), may hold values from -0.75 to 0.75
- output_down: bfloat16 [64, 16384], P(None, 'col'), may hold values from -0.046875 to 0.046875
- output_raise_map: bfloat16 [64, 16384], P(None, 'row'), may hold values from -0.75 to 0.75
Outputs:
- layer_output: float32 [512, 16384], P('dp', ('row', 'col'))
- input_grad: float32 [512, 16384], P('dp', ('row', 'col'))
- query_down_grad: float32 [64, 16384], P(None, 'row')
- query_raise_gradient: float32 [64, 16384], P(None, 'col')
- key_down_grad: float32 [64, 16384], P(None, 'row')
- key_raise_gradient: float32 [64, 1024], P(None, 'col')
- value_down_grad: float32 [64, 16384], P(None, 'row')
- value_raise_gradient: float32 [64, 1024], P(None, 'col')
- output_down_grad: float32 [64, 16384], P(None, 'col')
- output_raise_gradient: float32 [64, 16384], P(None, 'row')
The draws below stay inside these ranges and needn't reach their ends.
Inputs may be any that keep to these rules, and one draw needn't show every extreme that they name: `doc_ids`: each row is one replica's packed sequence; numbers never fall along a row.
All inputs are finite; a program needn't handle non-finite values.
Results may differ from the reference program's by a relative error of at most 0.04.
Values may be sent and summed in bfloat16 or wider, within the bound.
No kernel may reach another device: no remote copies, remote signals or barrier semaphores. Data moves between devices by JAX's collectives and lax.ppermute only.
A program may use at most 64 MiB of HBM per device.

```python
import math
import jax
import jax.numpy as jnp
import numpy as np
from jax import lax

D = 16384
H = 128
KVH = 8
DH = 128
R = 64
TOK = 256
HD = 16384
KVD = 1024
TOKENS = 512
N_DP = 2
N_ROW = 8
N_COL = 16


def shared_keys(key):
    return jnp.clip(jax.random.normal(key, (D, KVD), jnp.float32), -6.0, 6.0)


def draw_key_matrix(key, part):
    common = shared_keys(key)
    return (common * D ** (-0.5)).astype(jnp.bfloat16)


def draw_query_matrix(key, part):
    key = jax.random.fold_in(key, 23)
    own_part = jnp.clip(jax.random.normal(key, (D, HD), jnp.float32), -6.0, 6.0)
    return (own_part * D ** (-0.5)).astype(jnp.bfloat16)


def draw_hidden_input(key, part):
    key = jax.random.fold_in(key, 11)
    value_rows = jax.random.normal(jax.random.fold_in(key, 1), (TOKENS, D), jnp.float32)
    return jnp.clip(value_rows, -6.0, 6.0).astype(jnp.bfloat16)


def block_scale(own_key, extent, split, smallest, largest):
    gain = 1.0
    for position, parts in split:
        heights = jax.random.uniform(jax.random.fold_in(jax.random.fold_in(own_key, 6), position), (parts,), jnp.float32, smallest / len(split), largest / len(split))
        gain = gain * jnp.repeat(jnp.exp(heights), extent[position] // parts).reshape((-1,) + (1,) * (len(extent) - 1 - position))
    return gain


def profile(number_of, total, reach, skew):
    weights = [(1 << 20) // math.isqrt(grade ** skew) + 1 for grade in range(2, number_of + 1)]
    surplus, given = total - reach - (number_of - 1), [1] * (number_of - 1)
    while surplus > 0:
        movable = [i for i in range(number_of - 1) if given[i] < reach]
        mass, left = sum([weights[i] for i in movable]), surplus
        for i in movable:
            addition = min(reach - given[i], max(1, left * weights[i] // mass), surplus)
            given[i] = given[i] + addition
            surplus = surplus - addition
    return np.array([reach] + given)


def uneven(own_key, amount, total, limit, slope):
    if amount == 2:
        one = jax.random.randint(own_key, (), max(1, total - limit), min(limit, total - 1) + 1)
        return jnp.stack([one, total - one])
    sizes = jnp.asarray(profile(amount, total, limit, slope), jnp.int32)
    twos = (amount - 1) // 2
    source_of, taker = sizes[1:1 + 2 * twos:2], sizes[2:2 + 2 * twos:2]
    room = jnp.minimum(source_of - 1, limit - taker)
    shifted = jax.random.randint(jax.random.fold_in(own_key, 1), (twos,), 0, 1 << 20) % (room + 1)
    sizes = sizes.at[1:1 + 2 * twos:2].set(source_of - shifted).at[2:2 + 2 * twos:2].set(taker + shifted)
    return sizes[jax.random.permutation(jax.random.fold_in(own_key, 2), amount)]


def bell_draw(rng, dims, scale, reach, cuts=(), kind=jnp.bfloat16):
    level = block_scale(rng, dims, cuts, -0.22, 0.18) if cuts else 1.0
    drawn = jax.random.normal(rng, dims, jnp.float32) * scale * level
    return jnp.minimum(jnp.maximum(drawn, -reach), reach).astype(kind)


def setup_inputs(seed: int = 0) -> dict:
    key_of = jax.random.split(jax.random.key(seed), 16)
    return {
        "hidden_input": draw_hidden_input(jax.random.fold_in(key_of[15], 71), 0),
        "doc_ids": jax.vmap(lambda own: jnp.searchsorted(jnp.cumsum(uneven(own, max(TOK // 32, 4), TOK, TOK // 2, 0)), jnp.arange(TOK), side="right"))(jax.random.split(key_of[1], N_DP)).reshape((N_DP, TOK)).astype(jnp.int32),
        "cotangent": bell_draw(key_of[2], (TOKENS, D), 1.0, 6.0, ((0, 2), (1, 128))),
        "query_matrix": draw_query_matrix(jax.random.fold_in(key_of[15], 71), 0),
        "key_matrix": draw_key_matrix(jax.random.fold_in(key_of[15], 71), 0),
        "value_matrix": bell_draw(key_of[5], (D, KVD), D ** -0.5, 0.046875, ((0, 8), (1, 16))),
        "output_matrix": bell_draw(key_of[6], (HD, D), HD ** -0.5, 0.046875, ((0, 16), (1, 8))),
        "query_down": bell_draw(key_of[7], (R, D), D ** -0.5, 0.046875, ((1, 8),)),
        "query_raise_map": bell_draw(key_of[8], (R, HD), R ** -0.5, 0.75, ((1, 16),)),
        "key_down": bell_draw(key_of[9], (R, D), D ** -0.5, 0.046875, ((1, 8),)),
        "key_raise_map": bell_draw(key_of[10], (R, KVD), R ** -0.5, 0.75, ((1, 16),)),
        "value_down": bell_draw(key_of[11], (R, D), D ** -0.5, 0.046875, ((1, 8),)),
        "value_raise_map": bell_draw(key_of[12], (R, KVD), R ** -0.5, 0.75, ((1, 16),)),
        "output_down": bell_draw(key_of[13], (R, HD), HD ** -0.5, 0.046875, ((1, 16),)),
        "output_raise_map": bell_draw(key_of[14], (R, D), R ** -0.5, 0.75, ((1, 8),)),
    }


ADAPTER_SCALE = 0.5
ROPE_BASE = 500000.0


def matrix_product(left_side, right_side):
    return jnp.dot(left_side, right_side, preferred_element_type=jnp.float32)


def product(form, first_arg, second_arg):
    return jnp.einsum(form, first_arg.astype(jnp.float32), second_arg.astype(jnp.float32))


def rounded_back(value_rows):
    return lax.optimization_barrier(value_rows.astype(jnp.bfloat16)).astype(jnp.float32)


def block_split(left_side, right_side, block_count):
    block_width = left_side.shape[1] // block_count
    total = jnp.zeros((left_side.shape[0], right_side.shape[1]), jnp.float32)
    for block_index in range(block_count):
        block_span = slice(block_index * block_width, (block_index + 1) * block_width)
        total = total + rounded_back(matrix_product(left_side[:, block_span], right_side[block_span]))
    return total


def rope_tables(doc_row):
    length = doc_row.shape[0]
    places = jnp.arange(length, dtype=jnp.int32)
    same_doc = doc_row[:, None] == doc_row[None, :]
    doc_start = jnp.min(jnp.where(same_doc, places[None, :], length), axis=1).astype(jnp.int32)
    offsets = (places - doc_start).astype(jnp.float32)
    half_dim = DH // 2
    inverse = ROPE_BASE ** (-(jnp.arange(half_dim, dtype=jnp.float32) * 2.0 / DH))
    angles = offsets[:, None] * inverse[None, :]
    return jnp.cos(angles), jnp.sin(angles)


def rotate(vectors, cosine_rows, sine_rows):
    half_dim = vectors.shape[-1] // 2
    front_half = vectors[..., :half_dim]
    back_half = vectors[..., half_dim:]
    cosine_wide = cosine_rows[:, None, :]
    sine_wide = sine_rows[:, None, :]
    return jnp.concatenate([front_half * cosine_wide - back_half * sine_wide, back_half * cosine_wide + front_half * sine_wide], axis=-1)


def rotate_back(vectors, cosine_rows, sine_rows):
    half_dim = vectors.shape[-1] // 2
    front_half = vectors[..., :half_dim]
    back_half = vectors[..., half_dim:]
    cosine_wide = cosine_rows[:, None, :]
    sine_wide = sine_rows[:, None, :]
    return jnp.concatenate([front_half * cosine_wide + back_half * sine_wide, back_half * cosine_wide - front_half * sine_wide], axis=-1)


def attend(query_matrix_rows, key_rot, value_rank_rows, doc_row):
    query_total_count = query_matrix_rows.shape[0]
    query_places = jnp.arange(query_total_count, dtype=jnp.int32)
    key_places = jnp.arange(key_rot.shape[0], dtype=jnp.int32)
    allowed = (key_places[None, :] <= query_places[:, None]) & (doc_row[None, :] == doc_row[:, None])
    scores = product("qhd,kd->hqk", query_matrix_rows, key_rot) * (DH ** -0.5)
    scores = jnp.where(allowed[None, :, :], scores, -1e30)
    highest = jnp.max(scores, axis=-1, keepdims=True)
    weights = jnp.exp(scores - highest)
    normalized = weights / jnp.sum(weights, axis=-1, keepdims=True)
    mixed = product("hqk,kd->qhd", normalized.astype(jnp.bfloat16), value_rank_rows)
    return mixed, normalized


def attend_back(grad_low, normalized, query_matrix_rows, key_rot, value_rank_rows):
    normal_low = normalized.astype(jnp.bfloat16)
    value_gradients = product("hqk,qhd->kd", normal_low, grad_low)
    grad_weights = product("qhd,kd->hqk", grad_low, value_rank_rows)
    inner_sum = jnp.sum(normalized * grad_weights, axis=-1, keepdims=True)
    grad_scores = (normalized * (grad_weights - inner_sum) * (DH ** -0.5)).astype(jnp.bfloat16)
    query_gradients = product("hqk,kd->qhd", grad_scores, key_rot)
    key_gradients = product("hqk,qhd->kd", grad_scores, query_matrix_rows)
    return query_gradients, key_gradients, value_gradients


def reference(hidden_input, doc_ids, cotangent, query_matrix, key_matrix, value_matrix, output_matrix, query_down, query_raise_map, key_down, key_raise_map, value_down, value_raise_map, output_down, output_raise_map):
    query_rank_rows = matrix_product(hidden_input, query_down.T).astype(jnp.bfloat16)
    key_rank_rows = matrix_product(hidden_input, key_down.T).astype(jnp.bfloat16)
    value_rank_rows = matrix_product(hidden_input, value_down.T).astype(jnp.bfloat16)
    query_matrix_rows = block_split(hidden_input, query_matrix, N_ROW) + ADAPTER_SCALE * matrix_product(query_rank_rows, query_raise_map)
    key_rows = matrix_product(hidden_input, key_matrix) + ADAPTER_SCALE * matrix_product(key_rank_rows, key_raise_map)
    value_rows = (matrix_product(hidden_input, value_matrix) + ADAPTER_SCALE * matrix_product(value_rank_rows, value_raise_map)).astype(jnp.bfloat16)
    group_size = H // KVH
    saved = []
    attention_parts = []
    for replica in range(N_DP):
        row_span = slice(replica * TOK, (replica + 1) * TOK)
        doc_row = doc_ids[replica]
        cosine_rows, sine_rows = rope_tables(doc_row)
        query_rot = rotate(query_matrix_rows[row_span].reshape(TOK, H, DH), cosine_rows, sine_rows).astype(jnp.bfloat16)
        key_rot = rotate(key_rows[row_span].reshape(TOK, KVH, DH), cosine_rows, sine_rows).astype(jnp.bfloat16)
        value_heads = value_rows[row_span].reshape(TOK, KVH, DH)
        pieces = []
        probs_list = []
        for group in range(KVH):
            head_span = slice(group * group_size, (group + 1) * group_size)
            mixed, normalized = attend(query_rot[:, head_span], key_rot[:, group], value_heads[:, group], doc_row)
            pieces.append(mixed.astype(jnp.bfloat16))
            probs_list.append(normalized)
        attention_parts.append(jnp.concatenate(pieces, axis=1).reshape(TOK, HD))
        saved.append((cosine_rows, sine_rows, query_rot, key_rot, value_heads, probs_list))
    attention_result = jnp.concatenate(attention_parts, axis=0)
    output_rank_rows = matrix_product(attention_result, output_down.T).astype(jnp.bfloat16)
    layer_output = block_split(attention_result, output_matrix, N_COL) + ADAPTER_SCALE * matrix_product(output_rank_rows, output_raise_map)

    output_rank_gradient = (ADAPTER_SCALE * matrix_product(cotangent, output_raise_map.T)).astype(jnp.bfloat16)
    grad_attention = (block_split(cotangent, output_matrix.T, N_ROW) + matrix_product(output_rank_gradient, output_down)).astype(jnp.bfloat16)
    grad_query_parts = []
    grad_key_parts = []
    grad_value_parts = []
    for replica in range(N_DP):
        cosine_rows, sine_rows, query_rot, key_rot, value_heads, probs_list = saved[replica]
        grad_mixed = grad_attention[replica * TOK:(replica + 1) * TOK].reshape(TOK, H, DH)
        query_pieces = []
        key_pieces = []
        value_pieces = []
        for group in range(KVH):
            head_span = slice(group * group_size, (group + 1) * group_size)
            grad_query_rot, grad_key_rot, grad_value_sum = attend_back(grad_mixed[:, head_span], probs_list[group], query_rot[:, head_span], key_rot[:, group], value_heads[:, group])
            query_pieces.append(grad_query_rot)
            key_pieces.append(grad_key_rot)
            value_pieces.append(grad_value_sum)
        grad_query_rot = jnp.concatenate(query_pieces, axis=1)
        grad_key_rot = jnp.stack(key_pieces, axis=1)
        grad_query_parts.append(rotate_back(grad_query_rot, cosine_rows, sine_rows).astype(jnp.bfloat16).reshape(TOK, HD))
        grad_key_parts.append(rotate_back(grad_key_rot, cosine_rows, sine_rows).astype(jnp.bfloat16).reshape(TOK, KVD))
        grad_value_parts.append(jnp.stack(value_pieces, axis=1).astype(jnp.bfloat16).reshape(TOK, KVD))
    query_gradients = jnp.concatenate(grad_query_parts, axis=0)
    key_gradients = jnp.concatenate(grad_key_parts, axis=0)
    value_gradients = jnp.concatenate(grad_value_parts, axis=0)
    query_rank_gradient = (ADAPTER_SCALE * matrix_product(query_gradients, query_raise_map.T)).astype(jnp.bfloat16)
    key_rank_gradient = (ADAPTER_SCALE * matrix_product(key_gradients, key_raise_map.T)).astype(jnp.bfloat16)
    value_rank_gradient = (ADAPTER_SCALE * matrix_product(value_gradients, value_raise_map.T)).astype(jnp.bfloat16)
    query_block = HD // N_COL
    key_block = KVD // N_COL
    input_base = jnp.zeros((TOKENS, D), jnp.float32)
    for block_index in range(N_COL):
        query_span = slice(block_index * query_block, (block_index + 1) * query_block)
        key_span = slice(block_index * key_block, (block_index + 1) * key_block)
        block_term = (matrix_product(query_gradients[:, query_span], query_matrix[:, query_span].T)
                      + matrix_product(key_gradients[:, key_span], key_matrix[:, key_span].T)
                      + matrix_product(value_gradients[:, key_span], value_matrix[:, key_span].T))
        input_base = input_base + rounded_back(block_term)
    input_grad = (input_base + matrix_product(query_rank_gradient, query_down) + matrix_product(key_rank_gradient, key_down)
                  + matrix_product(value_rank_gradient, value_down))
    query_down_grad = matrix_product(query_rank_gradient.T, hidden_input)
    key_down_grad = matrix_product(key_rank_gradient.T, hidden_input)
    value_down_grad = matrix_product(value_rank_gradient.T, hidden_input)
    query_raise_gradient = ADAPTER_SCALE * matrix_product(query_rank_rows.T, query_gradients)
    key_raise_gradient = ADAPTER_SCALE * matrix_product(key_rank_rows.T, key_gradients)
    value_raise_gradient = ADAPTER_SCALE * matrix_product(value_rank_rows.T, value_gradients)
    output_down_grad = matrix_product(output_rank_gradient.T, attention_result)
    output_raise_gradient = ADAPTER_SCALE * matrix_product(output_rank_rows.T, cotangent)
    return (layer_output, input_grad, query_down_grad, query_raise_gradient, key_down_grad, key_raise_gradient,
            value_down_grad, value_raise_gradient, output_down_grad, output_raise_gradient)
```

```python
import jax
import jax.numpy as jnp
from jax import lax
from jax.sharding import PartitionSpec as P

KVH = 8
DH = 128


ADAPTER_SCALE = 0.5
ROPE_BASE = 500000.0


CORE = 1
PAIR = 1


def swapped(shard, axis, mask):
    return lax.ppermute(shard, axis, [(i, i ^ mask) for i in range(lax.axis_size(axis))])


def low(rows):
    return rows.astype(jnp.bfloat16)


def wide(rows):
    return rows.astype(jnp.float32)


def spread(shard, axis, unit):
    return [shard] + [swapped(shard, axis, k * unit) for k in (1, 2, 3)]


def in_order(shards, place):
    odd, upper = place & 1 == 1, place >> 1 & 1 == 1
    shards = [jnp.where(odd, shards[j ^ 1], shards[j]) for j in range(4)]
    return [jnp.where(upper, shards[j ^ 2], shards[j]) for j in range(4)]


def tree_sum(shards):
    return (wide(shards[0]) + wide(shards[1])) + (wide(shards[2]) + wide(shards[3]))


def block(array, index, size, dim):
    return lax.dynamic_slice_in_dim(array, index * size, size, dim)


def gather_columns(shard, y_index, zh_index):
    along_zh = jnp.concatenate(in_order(spread(shard, "col", 1), zh_index), axis=1)
    return jnp.concatenate(in_order(spread(along_zh, "col", 4), y_index), axis=1)


def scatter_columns(part_of, y_index, zh_index, sub_width):
    parts = [part_of(y_index ^ k) for k in range(4)]
    got = [swapped(low(parts[k]), "col", 4 * k) for k in (1, 2, 3)]
    mine = (parts[0] + wide(got[0])) + (wide(got[1]) + wide(got[2]))
    cells = [block(mine, zh_index ^ k, sub_width, 1) for k in range(4)]
    got = [swapped(low(cells[k]), "col", k) for k in (1, 2, 3)]
    return (cells[0] + wide(got[0])) + (wide(got[1]) + wide(got[2]))


def scatter_tokens(part, x_index, core_index):
    half = part.shape[0] // 2
    kept = wide(block(part, core_index, half, 0))
    kept = kept + wide(swapped(block(part, core_index ^ 1, half, 0), "row", CORE))
    size = half // 4
    cells = [block(kept, x_index ^ k, size, 0) for k in range(4)]
    got = [swapped(low(cells[k]), "row", 2 * k) for k in (1, 2, 3)]
    return (cells[0] + wide(got[0])) + (wide(got[1]) + wide(got[2]))


def gather_tokens(shard, x_index, core_index):
    half = jnp.concatenate(in_order(spread(shard, "row", 2), x_index), axis=0)
    other = swapped(half, "row", CORE)
    upper = core_index == 1
    return jnp.concatenate(
        [jnp.where(upper, other, half), jnp.where(upper, half, other)], axis=0
    )


def sum_row(part):
    pair_sum = low(wide(part) + wide(swapped(part, "row", CORE)))
    return tree_sum(spread(pair_sum, "row", 2))


def sum_column(part, y_index):
    size = part.shape[0] // 4
    cells = [block(part, y_index ^ k, size, 0) for k in range(4)]
    got = [cells[0]] + [swapped(cells[k], "col", 4 * k) for k in (1, 2, 3)]
    along_y = low(tree_sum(got))
    full = low(tree_sum(spread(along_y, "col", 1)))
    return jnp.concatenate(in_order(spread(full, "col", 4), y_index), axis=0)


def sum_replicas(part):
    part = low(part)
    return wide(part) + wide(swapped(part, "dp", 1))


def matrix_product(left_side, right_side):
    return jnp.dot(left_side, right_side, preferred_element_type=jnp.float32)


def product(form, first_arg, second_arg):
    return jnp.einsum(form, first_arg, second_arg, preferred_element_type=jnp.float32)


def rope_tables(doc_row):
    length = doc_row.shape[0]
    places = jnp.arange(length, dtype=jnp.int32)
    same_doc = doc_row[:, None] == doc_row[None, :]
    doc_start = jnp.min(jnp.where(same_doc, places[None, :], length), axis=1)
    offsets = (places - doc_start).astype(jnp.float32)
    half_dim = DH // 2
    inverse = ROPE_BASE ** (-(jnp.arange(half_dim, dtype=jnp.float32) * 2.0 / DH))
    angles = offsets[:, None] * inverse[None, :]
    return (jnp.cos(angles), jnp.sin(angles))


def rotate(vectors, cosine_rows, sine_rows):
    half_dim = vectors.shape[-1] // 2
    front_half = vectors[..., :half_dim]
    back_half = vectors[..., half_dim:]
    cosine_wide = cosine_rows[:, None, :]
    sine_wide = sine_rows[:, None, :]
    return jnp.concatenate(
        [
            front_half * cosine_wide - back_half * sine_wide,
            back_half * cosine_wide + front_half * sine_wide,
        ],
        axis=-1,
    )


def rotate_back(vectors, cosine_rows, sine_rows):
    half_dim = vectors.shape[-1] // 2
    front_half = vectors[..., :half_dim]
    back_half = vectors[..., half_dim:]
    cosine_wide = cosine_rows[:, None, :]
    sine_wide = sine_rows[:, None, :]
    return jnp.concatenate(
        [
            front_half * cosine_wide + back_half * sine_wide,
            back_half * cosine_wide - front_half * sine_wide,
        ],
        axis=-1,
    )


def attend(query_matrix_rows, key_rot, value_rank_rows, doc_row, first_row_index):
    query_total_count = query_matrix_rows.shape[0]
    query_places = first_row_index + jnp.arange(query_total_count, dtype=jnp.int32)
    key_places = jnp.arange(key_rot.shape[0], dtype=jnp.int32)
    query_docs = lax.dynamic_slice_in_dim(doc_row, first_row_index, query_total_count)
    allowed = (key_places[None, :] <= query_places[:, None]) & (
        doc_row[None, :] == query_docs[:, None]
    )
    scores = product("qhd,kd->hqk", query_matrix_rows, key_rot) * DH ** (-0.5)
    scores = jnp.where(allowed[None, :, :], scores, -1e30)
    highest = jnp.max(scores, axis=-1, keepdims=True)
    weights = jnp.exp(scores - highest)
    normalized = weights / jnp.sum(weights, axis=-1, keepdims=True)
    mixed = product("hqk,kd->qhd", normalized.astype(jnp.bfloat16), value_rank_rows)
    return (mixed, normalized)


def attend_back(grad_low, normalized, query_matrix_rows, key_rot, value_rank_rows):
    normal_low = normalized.astype(jnp.bfloat16)
    value_gradients = product("hqk,qhd->kd", normal_low, grad_low)
    grad_weights = product("qhd,kd->hqk", grad_low, value_rank_rows)
    inner_sum = jnp.sum(normalized * grad_weights, axis=-1, keepdims=True)
    grad_scores = (normalized * (grad_weights - inner_sum) * DH ** (-0.5)).astype(jnp.bfloat16)
    query_gradients = product("hqk,kd->qhd", grad_scores, key_rot)
    key_gradients = product("hqk,qhd->kd", grad_scores, query_matrix_rows)
    return (query_gradients, key_gradients, value_gradients)


def per_device(
    hidden_input,
    doc_ids,
    cotangent,
    query_matrix,
    key_matrix,
    value_matrix,
    output_matrix,
    query_down,
    query_raise_map,
    key_down,
    key_raise_map,
    value_down,
    value_raise_map,
    output_down,
    output_raise_map,
):
    row_index = lax.axis_index("row")
    col_index = lax.axis_index("col")
    x_index, core_index = row_index >> 1, row_index & 1
    y_index, zh_index = col_index >> 2, col_index & 3
    pair_upper = col_index & 1 == 1
    tokens, sub_width = hidden_input.shape
    rank = query_down.shape[0]
    key_width = key_matrix.shape[1]
    width = query_matrix.shape[1]
    heads = width // DH
    mine = tokens // lax.axis_size("row")
    first = core_index * (tokens // 2) + x_index * mine
    quarter = query_matrix.shape[0] // 4

    doc_row = doc_ids[0]
    cosine_rows, sine_rows = rope_tables(doc_row)
    cosine_mine = lax.dynamic_slice_in_dim(cosine_rows, first, mine, 0)
    sine_mine = lax.dynamic_slice_in_dim(sine_rows, first, mine, 0)

    hidden = gather_columns(hidden_input, y_index, zh_index)
    gradient = gather_columns(cotangent, y_index, zh_index)

    own_key = jnp.concatenate([key_matrix, key_raise_map], axis=0)
    own_value = jnp.concatenate([value_matrix, value_raise_map], axis=0)
    own_both = jnp.concatenate([own_key, own_value], axis=1)
    other_both = swapped(own_both, "col", PAIR)
    lower_both = jnp.where(pair_upper, other_both, own_both)
    upper_both = jnp.where(pair_upper, own_both, other_both)
    pair_both = jnp.concatenate(
        [
            lower_both[:, :key_width],
            upper_both[:, :key_width],
            lower_both[:, key_width:],
            upper_both[:, key_width:],
        ],
        axis=1,
    )
    depth = key_matrix.shape[0]
    pair_matrix = pair_both[:depth]
    key_raise_pair = pair_both[depth:, :DH]
    value_raise_pair = pair_both[depth:, DH:]
    downs = jnp.concatenate([query_down, key_down, value_down], axis=0)

    low_part = low(matrix_product(hidden, downs.T))
    key_value_part = matrix_product(hidden, pair_matrix) + ADAPTER_SCALE * jnp.concatenate(
        [
            matrix_product(low_part[:, rank : 2 * rank], key_raise_pair),
            matrix_product(low_part[:, 2 * rank :], value_raise_pair),
        ],
        axis=1,
    )
    key_value = sum_row(low(key_value_part))
    key_rot = low(rotate(key_value[:, None, :DH], cosine_rows, sine_rows))[:, 0, :]
    values = low(key_value[:, DH:])
    query_part = matrix_product(hidden, query_matrix) + ADAPTER_SCALE * matrix_product(
        low_part[:, :rank], query_raise_map
    )
    summed = scatter_tokens(
        jnp.concatenate([low(query_part), low_part], axis=1), x_index, core_index
    )
    query_rot = low(
        rotate(summed[:, :width].reshape(mine, heads, DH), cosine_mine, sine_mine)
    )
    mixed, normalized = attend(query_rot, key_rot, values, doc_row, first)
    attention_low = gather_tokens(
        jnp.concatenate([low(mixed).reshape(mine, width), low(summed[:, width:])], axis=1),
        x_index,
        core_index,
    )
    attention = attention_low[:, :width]
    down_low = attention_low[:, width:]

    out_low_part = low(matrix_product(attention, output_down.T))

    def layer_part(index):
        return matrix_product(
            attention, block(output_matrix, index, quarter, 1)
        ) + ADAPTER_SCALE * matrix_product(
            out_low_part, block(output_raise_map, index, quarter, 1)
        )

    layer_output = scatter_columns(layer_part, y_index, zh_index, sub_width)
    out_low = low(sum_column(out_low_part, y_index))
    out_raise_total = sum_replicas(ADAPTER_SCALE * matrix_product(out_low.T, gradient))

    out_grad_low_part = low(ADAPTER_SCALE * matrix_product(gradient, output_raise_map.T))
    grad_attention_part = matrix_product(gradient, output_matrix.T) + matrix_product(
        out_grad_low_part, output_down
    )
    grad_summed = scatter_tokens(
        jnp.concatenate([low(grad_attention_part), out_grad_low_part], axis=1),
        x_index,
        core_index,
    )
    grad_mixed = low(grad_summed[:, :width]).reshape(mine, heads, DH)
    grad_query_rot, grad_key_rot, grad_value_part = attend_back(
        grad_mixed, normalized, query_rot, key_rot, values
    )
    query_gradients = low(rotate_back(grad_query_rot, cosine_mine, sine_mine)).reshape(
        mine, width
    )
    grad_low = gather_tokens(
        jnp.concatenate([query_gradients, low(grad_summed[:, width:])], axis=1),
        x_index,
        core_index,
    )
    query_gradient = grad_low[:, :width]
    out_grad_low = grad_low[:, width:]
    grad_key_value = sum_row(low(jnp.concatenate([grad_key_rot, grad_value_part], axis=1)))
    key_gradient = low(
        rotate_back(grad_key_value[:, None, :DH], cosine_rows, sine_rows)[:, 0, :]
    )
    value_gradient = low(grad_key_value[:, DH:])
    key_value_gradient = jnp.concatenate([key_gradient, value_gradient], axis=1)

    raise_grad_part = low(
        ADAPTER_SCALE
        * jnp.concatenate(
            [
                matrix_product(query_gradient, query_raise_map.T),
                matrix_product(key_gradient, key_raise_pair.T),
                matrix_product(value_gradient, value_raise_pair.T),
            ],
            axis=1,
        )
    )

    def input_part(index):
        return (
            matrix_product(query_gradient, block(query_matrix, index, quarter, 0).T)
            + matrix_product(key_value_gradient, block(pair_matrix, index, quarter, 0).T)
            + matrix_product(raise_grad_part, block(downs, index, quarter, 1))
        )

    raise_grad = low(sum_column(raise_grad_part, y_index))
    input_grad = scatter_columns(input_part, y_index, zh_index, sub_width)

    other_hidden = swapped(hidden, "dp", 1)
    other_raise_grad = swapped(raise_grad, "dp", 1)
    down_total = matrix_product(raise_grad.T, hidden) + matrix_product(
        other_raise_grad.T, other_hidden
    )
    width_total = sum_replicas(
        jnp.concatenate(
            [
                ADAPTER_SCALE * matrix_product(down_low[:, :rank].T, query_gradient),
                matrix_product(out_grad_low.T, attention),
            ],
            axis=0,
        )
    )
    key_value_raise = ADAPTER_SCALE * jnp.concatenate(
        [
            matrix_product(down_low[:, rank : 2 * rank].T, key_gradient),
            matrix_product(down_low[:, 2 * rank :].T, value_gradient),
        ],
        axis=0,
    )
    lower_raise, upper_raise = key_value_raise[:, :key_width], key_value_raise[:, key_width:]
    kept = jnp.where(pair_upper, upper_raise, lower_raise)
    sent = jnp.where(pair_upper, lower_raise, upper_raise)
    kept = kept + swapped(sent, "col", PAIR)
    key_value_total = kept + swapped(kept, "dp", 1)
    return (
        layer_output,
        input_grad,
        down_total[:rank],
        width_total[:rank],
        down_total[rank : 2 * rank],
        key_value_total[:rank],
        down_total[2 * rank :],
        key_value_total[rank:],
        width_total[rank:],
        out_raise_total,
    )


def solution(mesh):
    in_specs = (
        P("dp", ("row", "col")),
        P("dp", None),
        P("dp", ("row", "col")),
        P("row", "col"),
        P("row", "col"),
        P("row", "col"),
        P("col", "row"),
        P(None, "row"),
        P(None, "col"),
        P(None, "row"),
        P(None, "col"),
        P(None, "row"),
        P(None, "col"),
        P(None, "col"),
        P(None, "row"),
    )
    out_specs = (
        P("dp", ("row", "col")),
        P("dp", ("row", "col")),
        P(None, "row"),
        P(None, "col"),
        P(None, "row"),
        P(None, "col"),
        P(None, "row"),
        P(None, "col"),
        P(None, "col"),
        P(None, "row"),
    )
    return jax.shard_map(
        per_device, mesh=mesh, in_specs=in_specs, out_specs=out_specs, check_vma=False
    )
```

```python
import functools

import jax
import jax.numpy as jnp
from jax import lax
from jax.experimental import pallas as pl
from jax.experimental.pallas import tpu as pltpu
from jax.sharding import PartitionSpec as P

DH = 128
HALF = DH // 2
ADAPTER_SCALE = 0.5
ROPE_BASE = 500000.0
CORE = 1
PAIR = 1


def swapped(shard, axis, mask):
    return lax.ppermute(shard, axis, [(i, i ^ mask) for i in range(lax.axis_size(axis))])


def low(rows):
    return rows.astype(jnp.bfloat16)


def wide(rows):
    return rows.astype(jnp.float32)


def matrix_product(left_side, right_side):
    return jnp.dot(left_side, right_side, preferred_element_type=jnp.float32)


def product(left_side, right_side, left_dim, right_dim):
    return lax.dot_general(
        left_side,
        right_side,
        (((left_dim,), (right_dim,)), ((), ())),
        preferred_element_type=jnp.float32,
    )


def spread(shard, axis, unit):
    return [shard] + [swapped(shard, axis, k * unit) for k in (1, 2, 3)]


def in_order(shards, place):
    odd, upper = place & 1 == 1, place >> 1 & 1 == 1
    shards = [jnp.where(odd, shards[j ^ 1], shards[j]) for j in range(4)]
    return [jnp.where(upper, shards[j ^ 2], shards[j]) for j in range(4)]


def tree_sum(shards):
    return (wide(shards[0]) + wide(shards[1])) + (wide(shards[2]) + wide(shards[3]))


def block(array, index, size, dim):
    return lax.dynamic_slice_in_dim(array, index * size, size, dim)


def two_halves(upper, own, other):
    return jnp.where(upper, other, own), jnp.where(upper, own, other)


def folded(rows, parts):
    return jnp.concatenate(jnp.split(rows, parts, axis=0), axis=1)


def unfolded(rows, parts):
    return jnp.concatenate(jnp.split(rows, parts, axis=1), axis=0)


def sum_replicas(part):
    part = low(part)
    return wide(part) + wide(swapped(part, "dp", 1))


def rope_tables(doc_row):
    length = doc_row.shape[0]
    places = jnp.arange(length, dtype=jnp.int32)
    same_doc = doc_row[:, None] == doc_row[None, :]
    doc_start = jnp.min(jnp.where(same_doc, places[None, :], length), axis=1)
    offsets = (places - doc_start).astype(jnp.float32)
    inverse = ROPE_BASE ** (-(jnp.arange(HALF, dtype=jnp.float32) * 2.0 / DH))
    angles = offsets[:, None] * inverse[None, :]
    cosine, sine = jnp.cos(angles), jnp.sin(angles)
    return (
        jnp.concatenate([cosine, cosine], axis=1),
        jnp.concatenate([-sine, sine], axis=1),
    )


def row_slice(start, size):
    return pl.ds(pl.multiple_of(start, size), size)


def kernel_call(kernel, out_shape, operands, scratch=(), flops=0, name=None):
    vmem = pl.BlockSpec(memory_space=pltpu.VMEM)
    smem = pl.BlockSpec(memory_space=pltpu.SMEM)
    return pl.pallas_call(
        kernel,
        out_shape=out_shape,
        in_specs=[smem] + [vmem] * (len(operands) - 1),
        out_specs=jax.tree.map(lambda _: vmem, out_shape),
        scratch_shapes=list(scratch),
        compiler_params=pltpu.CompilerParams(vmem_limit_bytes=40 << 20),
        cost_estimate=pl.CostEstimate(
            flops=flops, bytes_accessed=2 << 20, transcendentals=0
        ),
        name=name,
    )(*operands)


Y_BLOCK, ZH_BLOCK, X_BLOCK, CORE_AT, PAIR_AT = 0, 4, 8, 12, 13


def part_rows(index, k, size):
    return row_slice(index[Y_BLOCK + k] * size, size)


def split_rows(index, rows, width, sent, kept):
    half = sent.shape[0]
    core = index[CORE_AT]
    for ref, place in ((sent, 1 - core), (kept, core)):
        ref[:, :width] = low(rows[row_slice(place * half, half), :])


def project_kernel(
    index, h0, h1, h2, h3, query, pair, downs, query_raise, side_raise, sent, kept, q, lo
):
    blocks = (h0, h1, h2, h3)
    size = h0.shape[1]
    cuts = [part_rows(index, k, size) for k in range(4)]
    low_rows = sum(product(blocks[k][...], downs[:, cuts[k]], 1, 1) for k in range(4))
    lo[...] = low_rows
    low_rows = low(low_rows)
    key_value = sum(matrix_product(blocks[k][...], pair[cuts[k], :]) for k in range(4))
    key_value = low(key_value + ADAPTER_SCALE * matrix_product(low_rows, side_raise[...]))
    q[...] = ADAPTER_SCALE * matrix_product(low_rows, query_raise[...]) + sum(
        matrix_product(blocks[k][...], query[cuts[k], :]) for k in range(4)
    )
    half, width = sent.shape[0], q.shape[1]
    split_rows(index, q, width, sent, kept)
    split_rows(index, lo, lo.shape[1], sent.at[:, width + 2 * DH :], kept.at[:, width + 2 * DH :])
    for ref in (sent, kept):
        ref[:, width : width + DH] = key_value[:half]
        ref[:, width + DH : width + 2 * DH] = key_value[half:]


def project_back_kernel(
    index, g0, g1, g2, g3, output, output_raise, output_down, sent, kept, g, lo
):
    blocks = (g0, g1, g2, g3)
    size = g0.shape[1]
    cuts = [part_rows(index, k, size) for k in range(4)]
    low_rows = ADAPTER_SCALE * sum(
        product(blocks[k][...], output_raise[:, cuts[k]], 1, 1) for k in range(4)
    )
    lo[...] = low_rows[:, DH:]
    g[...] = matrix_product(low(low_rows), output_down[...]) + sum(
        product(blocks[k][...], output[:, cuts[k]], 1, 1) for k in range(4)
    )
    width = g.shape[1]
    split_rows(index, g, width, sent, kept)
    split_rows(index, lo, DH, sent.at[:, width:], kept.at[:, width:])


def cells_kernel(fold, index, kept, got, c0, c1, c2, c3, total):
    total[...] = wide(kept[...]) + wide(got[...])
    mine = c0.shape[0]
    first, last = fold
    for k, cell in enumerate((c0, c1, c2, c3)):
        rows = row_slice(index[X_BLOCK + k] * mine, mine)
        cell[:, :first] = low(total[rows, :first])
        size = last - first
        for j in range(4 if size else 0):
            cell[:, first + j * size : first + (j + 1) * size] = low(
                total[j * mine : (j + 1) * mine, first:last]
            )
        cell[:, first + 4 * size :] = low(total[rows, last:])


def attend_kernel(
    index,
    own_ref,
    first_ref,
    second_ref,
    third_ref,
    own_side,
    other_side,
    cosine_ref,
    sine_ref,
    cosine_mine_ref,
    sine_mine_ref,
    allowed_ref,
    message_ref,
    probs_ref,
    query_ref,
    key_ref,
    value_ref,
):
    refs = (own_ref, first_ref, second_ref, third_ref)
    mine = cosine_mine_ref.shape[0]
    tokens = cosine_ref.shape[0]
    heads = query_ref.shape[0] // mine
    width = heads * DH
    chunks = tokens // mine

    def total(start, size):
        return tree_sum([ref[:, start : start + size] for ref in refs])

    in_front = lax.broadcasted_iota(jnp.int32, (mine, DH), 1) < HALF
    pair_upper = jnp.full((mine, DH), index[PAIR_AT], jnp.int32) > 0
    for chunk in range(chunks):
        row = (chunk % 2) * (tokens // 2) + (chunk // 2) * mine
        own = wide(own_side[:, chunk * DH : (chunk + 1) * DH])
        other = wide(other_side[:, chunk * DH : (chunk + 1) * DH])
        lower = jnp.where(pair_upper, other, own)
        upper = jnp.where(pair_upper, own, other)
        keys = jnp.where(in_front, lower, pltpu.roll(upper, HALF, 1))
        values = jnp.where(in_front, pltpu.roll(lower, HALF, 1), upper)
        rows = slice(row, row + mine)
        turned = keys * cosine_ref[rows, :] + pltpu.roll(keys, HALF, 1) * sine_ref[rows, :]
        key_ref[rows, :] = low(turned)
        value_ref[rows, :] = low(values)
    cosine, sine = cosine_mine_ref[...], sine_mine_ref[...]
    for head in range(heads):
        queries = total(head * DH, DH)
        turned = queries * cosine + pltpu.roll(queries, HALF, 1) * sine
        query_ref[head * mine : (head + 1) * mine, :] = low(turned)
    scores = product(query_ref[...], key_ref[...], 1, 1) * DH ** (-0.5)
    allowed = jnp.concatenate([allowed_ref[...]] * heads, axis=0) > 0.0
    scores = jnp.where(allowed, scores, -1e30)
    weights = jnp.exp(scores - jnp.max(scores, axis=-1, keepdims=True))
    probs = weights / jnp.sum(weights, axis=-1, keepdims=True)
    probs_ref[...] = probs
    mixed = low(matrix_product(low(probs), value_ref[...]))
    for head in range(heads):
        message_ref[:, head * DH : (head + 1) * DH] = mixed[head * mine : (head + 1) * mine]
    tail = width + DH * chunks
    message_ref[:, width:] = low(total(tail, own_ref.shape[1] - tail))


def attend_back_kernel(
    index,
    own_ref,
    first_ref,
    second_ref,
    third_ref,
    probs_ref,
    query_ref,
    key_ref,
    value_ref,
    cosine_ref,
    sine_ref,
    cosine_mine_ref,
    sine_mine_ref,
    message_ref,
    side_kept,
    side_sent,
    grad_ref,
):
    refs = (own_ref, first_ref, second_ref, third_ref)
    mine = cosine_mine_ref.shape[0]
    tokens = cosine_ref.shape[0]
    heads = query_ref.shape[0] // mine
    width = heads * DH

    def total(start, size):
        return tree_sum([ref[:, start : start + size] for ref in refs])

    for head in range(heads):
        grad_ref[head * mine : (head + 1) * mine, :] = low(total(head * DH, DH))
    grads = grad_ref[...]
    probs = probs_ref[...]
    grad_probs = product(grads, value_ref[...], 1, 1)
    inner = jnp.sum(probs * grad_probs, axis=-1, keepdims=True)
    grad_scores = low(probs * (grad_probs - inner) * DH ** (-0.5))
    keys = product(grad_scores, query_ref[...], 0, 0)
    keys = keys * cosine_ref[...] - pltpu.roll(keys, HALF, 1) * sine_ref[...]
    values = product(low(probs), grads, 0, 0)
    in_front = lax.broadcasted_iota(jnp.int32, (tokens, DH), 1) < HALF
    pair_upper = jnp.full((tokens, DH), index[PAIR_AT], jnp.int32) > 0
    lower = jnp.where(in_front, keys, pltpu.roll(values, HALF, 1))
    upper = jnp.where(in_front, pltpu.roll(keys, HALF, 1), values)
    kept = low(jnp.where(pair_upper, upper, lower))
    sent = low(jnp.where(pair_upper, lower, upper))
    for j in range(tokens // mine):
        side_kept[:, j * DH : (j + 1) * DH] = kept[j * mine : (j + 1) * mine]
        side_sent[:, j * DH : (j + 1) * DH] = sent[j * mine : (j + 1) * mine]
    queries = matrix_product(grad_scores, key_ref[...])
    cosine, sine = cosine_mine_ref[...], sine_mine_ref[...]
    for head in range(heads):
        rows = queries[head * mine : (head + 1) * mine]
        turned = rows * cosine - pltpu.roll(rows, HALF, 1) * sine
        message_ref[:, head * DH : (head + 1) * DH] = low(turned)
    message_ref[:, width:] = low(total(width, own_ref.shape[1] - width))


def join_kernel(index, s0, s1, s2, s3, joined):
    shards = (s0, s1, s2, s3)
    mine = s0.shape[0]
    width = s0.shape[1] - 9 * DH
    for k, shard in enumerate(shards):
        rows = slice(k * mine, (k + 1) * mine)
        joined[rows, :width] = shard[:, :width]
        for half in range(2):
            start = width + (k + 4 * half) * DH
            joined[rows, width + half * DH : width + (half + 1) * DH] = low(
                tree_sum([each[:, start : start + DH] for each in shards])
            )
        joined[rows, width + 2 * DH :] = shard[:, width + 8 * DH :]


def place_rows(index, own, got, target):
    half = own.shape[0]
    mine = half // 4
    core = index[CORE_AT]
    for source, place in ((own, core), (got, 1 - core)):
        for k in range(4):
            start = place * half + index[X_BLOCK + k] * mine
            target[row_slice(start, mine), :] = source[k * mine : (k + 1) * mine, :]


def input_kernel(
    index,
    own,
    got,
    own_attention,
    got_attention,
    query,
    pair,
    downs,
    query_raise,
    side_raise,
    output_down,
    p0,
    p1,
    p2,
    p3,
    low_cell,
    rows_low,
    out_low,
    grads,
    key_value,
    low_sums,
):
    width = query.shape[1]
    size = p0.shape[1]
    tokens = key_value.shape[0]
    half = tokens // 2
    place_rows(index, own.at[:, :width], got.at[:, :width], grads.at[:, :width])
    place_rows(
        index, own.at[:, width + 2 * DH :], got.at[:, width + 2 * DH :], grads.at[:, width:]
    )
    place_rows(index, own_attention, got_attention, rows_low)
    side = low(wide(own[:, width : width + 2 * DH]) + wide(got[:, width : width + 2 * DH]))
    key_value[:half] = side[:, :DH]
    key_value[half:] = side[:, DH:]
    out_low[...] = low(product(rows_low[:, :width], output_down[...], 1, 1))
    raised = product(grads[:, :width], query_raise[...], 1, 1) + product(
        key_value[...], side_raise[...], 1, 1
    )
    low_sums[...] = low(ADAPTER_SCALE * raised + wide(out_low[...]))
    cut = tokens // 4
    for k, ref in enumerate((p0, p1, p2, p3)):
        rows = part_rows(index, k, size)
        part = (
            product(grads[:, :width], query[rows, :], 1, 1)
            + product(key_value[...], pair[rows, :], 1, 1)
            + matrix_product(low_sums[...], downs[:, rows])
        )
        ref[:tokens, :] = part.astype(ref.dtype)
        low_rows = low_sums[row_slice(index[Y_BLOCK + k] * cut, cut), :]
        target = ref.at[tokens:, :] if k else low_cell
        lows = low_rows.shape[1]
        target[:, :lows] = low_rows[: cut // 2]
        target[:, lows:] = low_rows[cut // 2 :]


def layer_kernel(
    index,
    rows_low,
    out_low,
    grads,
    key_value,
    output,
    output_raise,
    p0,
    p1,
    p2,
    p3,
    width_part,
):
    width = output.shape[0]
    size = p0.shape[1]
    for k, ref in enumerate((p0, p1, p2, p3)):
        columns = part_rows(index, k, size)
        part = matrix_product(
            rows_low[:, :width], output[:, columns]
        ) + ADAPTER_SCALE * matrix_product(out_low[...], output_raise[:, columns])
        ref[...] = part.astype(ref.dtype)
    by_query = ADAPTER_SCALE * product(rows_low[:, width:], grads[:, :width], 0, 0)
    by_side = ADAPTER_SCALE * product(rows_low[:, width:], key_value[...], 0, 0)
    by_output = product(grads[:, width:], rows_low[:, :width], 0, 0)
    rank = DH // 2
    width_part[:rank, :width] = low(by_query[:rank])
    width_part[rank:, :width] = low(by_output[rank:])
    width_part[:, width:] = low(by_side[rank : 3 * rank])


def narrow_kernel(index, own, low_own, g1, g2, g3, c0, c1, c2, c3, low_mine, total):
    tokens, size = c0.shape
    total[...] = (own[...] + wide(g1[:tokens, :])) + (
        wide(g2[:tokens, :]) + wide(g3[:tokens, :])
    )
    if low_own is not None:
        sums = low(
            tree_sum([low_own[...], g1[tokens:, :], g2[tokens:, :], g3[tokens:, :]])
        )
        cut = sums.shape[0]
        for k in range(4):
            low_mine[k * cut : (k + 1) * cut, :] = sums[:, k * size : (k + 1) * size]
    for k, ref in enumerate((c0, c1, c2, c3)):
        cell = total[:, row_slice(index[ZH_BLOCK + k] * size, size)]
        ref[:tokens, :] = cell.astype(ref.dtype)
        if low_own is not None and k:
            ref[tokens:, :] = low_mine[...]


def plain_narrow_kernel(index, own, g1, g2, g3, c0, c1, c2, c3, total):
    narrow_kernel(index, own, None, g1, g2, g3, c0, c1, c2, c3, None, total)


def down_kernel(index, *refs):
    hidden, gradient, other = refs[:4], refs[4:8], refs[8:12]
    low_rows, other_low = refs[12:14]
    outs = refs[14:18]
    rank = outs[0].shape[0]
    tokens, size = hidden[0].shape
    own_left = low(wide(low_rows[...]).T)
    other_left = low(wide(other_low[...]).T)
    cut = 3 * rank
    for k in range(4):
        columns = row_slice(index[Y_BLOCK + k] * size, size)
        down = matrix_product(own_left[:cut], hidden[k][...]) + matrix_product(
            other_left[:cut], other[k][:tokens, :]
        )
        raised = ADAPTER_SCALE * (
            matrix_product(own_left[cut:], gradient[k][...])
            + matrix_product(other_left[cut:], other[k][tokens:, :])
        )
        for j in range(3):
            outs[j][:, columns] = down[j * rank : (j + 1) * rank]
        outs[3][:, columns] = raised


def per_device(
    hidden_input,
    doc_ids,
    cotangent,
    query_matrix,
    key_matrix,
    value_matrix,
    output_matrix,
    query_down,
    query_raise_map,
    key_down,
    key_raise_map,
    value_down,
    value_raise_map,
    output_down,
    output_raise_map,
):
    row_index = lax.axis_index("row")
    col_index = lax.axis_index("col")
    x_index, core_index = row_index >> 1, row_index & 1
    y_index, zh_index = col_index >> 2, col_index & 3
    index = jnp.stack(
        [y_index ^ k for k in range(4)]
        + [zh_index ^ k for k in range(4)]
        + [x_index ^ k for k in range(4)]
        + [core_index, col_index & 1]
    ).astype(jnp.int32)
    tokens, sub_width = hidden_input.shape
    half = tokens // 2
    rank = query_down.shape[0]
    depth, width = query_matrix.shape
    mine = tokens // lax.axis_size("row")
    first = core_index * half + x_index * mine
    quarter = depth // 4
    heads_rows = width // DH * mine
    shape = jax.ShapeDtypeStruct
    short, full = jnp.bfloat16, jnp.float32

    hidden_z = spread(hidden_input, "col", 1)
    gradient_z = spread(cotangent, "col", 1)
    hidden_zh = jnp.concatenate(in_order(hidden_z, zh_index), axis=1)
    hidden_y = spread(hidden_zh, "col", 4)
    gradient_zh = jnp.concatenate(in_order(gradient_z, zh_index), axis=1)
    gradient_y = spread(gradient_zh, "col", 4)
    both = swapped(jnp.concatenate([hidden_zh, gradient_zh], axis=0), "dp", 1)

    (
        doc_row,
        key_matrix,
        value_matrix,
        query_down,
        query_raise_map,
        key_down,
        key_raise_map,
        value_down,
        value_raise_map,
        output_down,
        output_raise_map,
        _,
    ) = lax.optimization_barrier(
        (
            doc_ids[0],
            key_matrix,
            value_matrix,
            query_down,
            query_raise_map,
            key_down,
            key_raise_map,
            value_down,
            value_raise_map,
            output_down,
            output_raise_map,
            hidden_zh,
        )
    )
    cosine, sine = rope_tables(doc_row)
    tables = (
        cosine,
        sine,
        lax.dynamic_slice_in_dim(cosine, first, mine, 0),
        lax.dynamic_slice_in_dim(sine, first, mine, 0),
    )
    places = jnp.arange(tokens, dtype=jnp.int32)
    my_docs = lax.dynamic_slice_in_dim(doc_row, first, mine)
    my_places = first + jnp.arange(mine, dtype=jnp.int32)
    allowed = wide(
        (places[None, :] <= my_places[:, None]) & (doc_row[None, :] == my_docs[:, None])
    )
    pair_matrix = jnp.concatenate([key_matrix, value_matrix], axis=1)

    def zeros(rows, columns):
        return jnp.zeros((rows, columns), short)

    downs = jnp.concatenate([query_down, key_down, value_down, zeros(rank, depth)], axis=0)
    query_raise = jnp.concatenate([query_raise_map, zeros(3 * rank, width)], axis=0)
    nothing = zeros(rank, rank)
    side_raise = jnp.concatenate(
        [
            zeros(rank, 2 * rank),
            jnp.concatenate([key_raise_map, nothing], axis=1),
            jnp.concatenate([nothing, value_raise_map], axis=1),
            zeros(rank, 2 * rank),
        ],
        axis=0,
    )
    output_down_low = jnp.concatenate([zeros(3 * rank, width), output_down], axis=0)
    output_raise = jnp.concatenate([zeros(3 * rank, depth), output_raise_map], axis=0)
    lows = 4 * rank

    columns = width + 2 * DH + lows
    sent, kept = kernel_call(
        project_kernel,
        (shape((half, columns), short),) * 2,
        (index, *hidden_y, query_matrix, pair_matrix, downs, query_raise, side_raise),
        scratch=[pltpu.VMEM((tokens, width), full), pltpu.VMEM((tokens, lows), full)],
        flops=2 * tokens * depth * columns,
        name="project",
    )
    columns = width + 8 * DH + lows
    cells = kernel_call(
        functools.partial(cells_kernel, (width, width + 2 * DH)),
        (shape((mine, columns), short),) * 4,
        (index, kept, swapped(sent, "row", CORE)),
        scratch=[pltpu.VMEM(sent.shape, full)],
        name="cells",
    )
    cells = [cells[0]] + [swapped(cells[k], "row", 2 * k) for k in (1, 2, 3)]
    side = low(tree_sum([cell[:, width : width + 8 * DH] for cell in cells]))
    message, *saved = kernel_call(
        attend_kernel,
        (
            shape((mine, width + lows), short),
            shape((heads_rows, tokens), full),
            shape((heads_rows, DH), short),
            shape((tokens, DH), short),
            shape((tokens, DH), short),
        ),
        (index, *cells, side, swapped(side, "col", PAIR), *tables, allowed),
        flops=4 * heads_rows * tokens * DH,
        name="attend",
    )
    attention = jnp.concatenate(spread(message, "row", 2), axis=0)
    got_attention = swapped(attention, "row", CORE)

    gradient_y[0], both = lax.optimization_barrier((gradient_y[0], both))
    sent, kept = kernel_call(
        project_back_kernel,
        (shape((half, width + DH), short),) * 2,
        (index, *gradient_y, output_matrix, output_raise, output_down_low),
        scratch=[pltpu.VMEM((tokens, width), full), pltpu.VMEM((tokens, DH), full)],
        flops=2 * tokens * depth * width,
        name="project_back",
    )
    cells = kernel_call(
        functools.partial(cells_kernel, (width, width)),
        (shape((mine, width + DH), short),) * 4,
        (index, kept, swapped(sent, "row", CORE)),
        scratch=[pltpu.VMEM(sent.shape, full)],
        name="cells_back",
    )
    cells = [cells[0]] + [swapped(cells[k], "row", 2 * k) for k in (1, 2, 3)]
    other_y = spread(both, "col", 4)
    cells[0], other_y[1], other_y[2], other_y[3] = lax.optimization_barrier(
        (cells[0], other_y[1], other_y[2], other_y[3])
    )
    message, side_kept, side_sent = kernel_call(
        attend_back_kernel,
        (
            shape((mine, width + DH), short),
            shape((mine, 8 * DH), short),
            shape((mine, 8 * DH), short),
        ),
        (index, *cells, *saved, *tables),
        scratch=[pltpu.VMEM((heads_rows, DH), short)],
        flops=8 * heads_rows * tokens * DH,
        name="attend_back",
    )
    side = low(wide(side_kept) + wide(swapped(side_sent, "col", PAIR)))
    message = jnp.concatenate([message[:, :width], side, message[:, width:]], axis=1)
    joined = kernel_call(
        join_kernel,
        shape((half, width + 3 * DH), short),
        (index, *spread(message, "row", 2)),
        name="join",
    )
    *parts, low_cell, rows_low, out_low, grads, key_value = kernel_call(
        input_kernel,
        (
            shape((tokens, quarter), full),
            *[shape((tokens + tokens // 8, quarter), short)] * 3,
            shape((tokens // 8, quarter), short),
            shape((tokens, width + lows), short),
            shape((tokens, lows), short),
            shape((tokens, width + DH), short),
            shape((tokens, DH), short),
        ),
        (
            index,
            joined,
            swapped(joined, "row", CORE),
            attention,
            got_attention,
            query_matrix,
            pair_matrix,
            downs,
            query_raise,
            side_raise,
            output_down_low,
        ),
        scratch=[pltpu.VMEM((tokens, lows), short)],
        flops=2 * tokens * depth * width,
        name="input",
    )
    got_input = [swapped(parts[k], "col", 4 * k) for k in (1, 2, 3)]
    *layer_parts, width_part = kernel_call(
        layer_kernel,
        (
            shape((tokens, quarter), full),
            *[shape((tokens, quarter), short)] * 3,
            shape((2 * rank, width + DH), short),
        ),
        (index, rows_low, out_low, grads, key_value, output_matrix, output_raise),
        flops=2 * tokens * depth * width,
        name="layer",
    )
    got_layer = [swapped(layer_parts[k], "col", 4 * k) for k in (1, 2, 3)]
    width_total = sum_replicas(width_part)
    *cells, low_mine = kernel_call(
        narrow_kernel,
        (
            shape((tokens, sub_width), full),
            *[shape((tokens + half, sub_width), short)] * 3,
            shape((half, sub_width), short),
        ),
        (index, parts[0], low_cell, *got_input),
        scratch=[pltpu.VMEM((tokens, quarter), full)],
        name="narrow_input",
    )
    got = [swapped(cells[k], "col", k) for k in (1, 2, 3)]
    layer_cells = kernel_call(
        plain_narrow_kernel,
        (shape((tokens, sub_width), full), *[shape((tokens, sub_width), short)] * 3),
        (index, layer_parts[0], *got_layer),
        scratch=[pltpu.VMEM((tokens, quarter), full)],
        name="narrow_layer",
    )
    got_layer = [swapped(layer_cells[k], "col", k) for k in (1, 2, 3)]
    low_mine = folded(low(tree_sum([low_mine] + [part[tokens:] for part in got])), 4)
    low_rows = jnp.concatenate(
        [unfolded(rows, 2) for rows in in_order(spread(low_mine, "col", 4), y_index)], axis=0
    )
    input_grad = (cells[0] + wide(got[0][:tokens])) + (
        wide(got[1][:tokens]) + wide(got[2][:tokens])
    )
    layer_output = (layer_cells[0] + wide(got_layer[0])) + (
        wide(got_layer[1]) + wide(got_layer[2])
    )

    downs_total = kernel_call(
        down_kernel,
        (shape((rank, depth), full),) * 4,
        (index, *hidden_y, *gradient_y, *other_y, low_rows, swapped(low_rows, "dp", 1)),
        flops=4 * tokens * depth * lows,
        name="down_grads",
    )
    return (
        layer_output,
        input_grad,
        downs_total[0],
        width_total[:rank, :width],
        downs_total[1],
        width_total[:rank, width : width + rank],
        downs_total[2],
        width_total[rank:, width + rank :],
        width_total[rank:, :width],
        downs_total[3],
    )


def solution(mesh):
    in_specs = (
        P("dp", ("row", "col")),
        P("dp", None),
        P("dp", ("row", "col")),
        P("row", "col"),
        P("row", "col"),
        P("row", "col"),
        P("col", "row"),
        P(None, "row"),
        P(None, "col"),
        P(None, "row"),
        P(None, "col"),
        P(None, "row"),
        P(None, "col"),
        P(None, "col"),
        P(None, "row"),
    )
    out_specs = (
        P("dp", ("row", "col")),
        P("dp", ("row", "col")),
        P(None, "row"),
        P(None, "col"),
        P(None, "row"),
        P(None, "col"),
        P(None, "row"),
        P(None, "col"),
        P(None, "col"),
        P(None, "row"),
    )
    return jax.shard_map(
        per_device, mesh=mesh, in_specs=in_specs, out_specs=out_specs, check_vma=False
    )
```

```python
import functools

import jax
import jax.numpy as jnp
from jax import lax
from jax.experimental import pallas as pl
from jax.experimental.pallas import tpu as pltpu
from jax.sharding import PartitionSpec as P

DH = 128
HALF = DH // 2
ADAPTER_SCALE = 0.5
ROPE_BASE = 500000.0
CORE = 1
PAIR = 1


def swapped(shard, axis, mask):
    return lax.ppermute(shard, axis, [(i, i ^ mask) for i in range(lax.axis_size(axis))])


def low(rows):
    return rows.astype(jnp.bfloat16)


def wide(rows):
    return rows.astype(jnp.float32)


def matrix_product(left_side, right_side):
    return jnp.dot(left_side, right_side, preferred_element_type=jnp.float32)


def product(left_side, right_side, left_dim, right_dim):
    return lax.dot_general(
        left_side,
        right_side,
        (((left_dim,), (right_dim,)), ((), ())),
        preferred_element_type=jnp.float32,
    )


def spread(shard, axis, unit):
    return [shard] + exchanged([shard] * 4, axis, unit)


def exchanged(shards, axis, unit):
    got = {k: swapped(shards[k], axis, k * unit) for k in (2, 1, 3)}
    return [got[k] for k in (1, 2, 3)]


def in_order(shards, place):
    odd, upper = place & 1 == 1, place >> 1 & 1 == 1
    shards = [jnp.where(odd, shards[j ^ 1], shards[j]) for j in range(4)]
    return [jnp.where(upper, shards[j ^ 2], shards[j]) for j in range(4)]


def tree_sum(shards):
    return (wide(shards[0]) + wide(shards[1])) + (wide(shards[2]) + wide(shards[3]))


def block(array, index, size, dim):
    return lax.dynamic_slice_in_dim(array, index * size, size, dim)


def two_halves(upper, own, other):
    return jnp.where(upper, other, own), jnp.where(upper, own, other)


def folded(rows, parts):
    return jnp.concatenate(jnp.split(rows, parts, axis=0), axis=1)


def unfolded(rows, parts):
    return jnp.concatenate(jnp.split(rows, parts, axis=1), axis=0)


def sum_replicas(part):
    part = low(part)
    return wide(part) + wide(swapped(part, "dp", 1))


def rope_tables(doc_row):
    length = doc_row.shape[0]
    places = jnp.arange(length, dtype=jnp.int32)
    same_doc = doc_row[:, None] == doc_row[None, :]
    doc_start = jnp.min(jnp.where(same_doc, places[None, :], length), axis=1)
    offsets = (places - doc_start).astype(jnp.float32)
    inverse = ROPE_BASE ** (-(jnp.arange(HALF, dtype=jnp.float32) * 2.0 / DH))
    angles = offsets[:, None] * inverse[None, :]
    cosine, sine = jnp.cos(angles), jnp.sin(angles)
    return (
        jnp.concatenate([cosine, cosine], axis=1),
        jnp.concatenate([-sine, sine], axis=1),
    )


def row_slice(start, size):
    return pl.ds(pl.multiple_of(start, size), size)


def far_first(shards):
    return [*shards[:-3], shards[-2], shards[-3], shards[-1]]


def kernel_call(kernel, out_shape, operands, scratch=(), flops=0, name=None):
    vmem = pl.BlockSpec(memory_space=pltpu.VMEM)
    smem = pl.BlockSpec(memory_space=pltpu.SMEM)
    return pl.pallas_call(
        kernel,
        out_shape=out_shape,
        in_specs=[smem] + [vmem] * (len(operands) - 1),
        out_specs=jax.tree.map(lambda _: vmem, out_shape),
        scratch_shapes=list(scratch),
        compiler_params=pltpu.CompilerParams(vmem_limit_bytes=14 << 20),
        cost_estimate=pl.CostEstimate(
            flops=flops, bytes_accessed=2 << 20, transcendentals=0
        ),
        name=name,
    )(*operands)


Y_BLOCK, ZH_BLOCK, X_BLOCK, CORE_AT, PAIR_AT = 0, 4, 8, 12, 13


def part_rows(index, k, size):
    return row_slice(index[Y_BLOCK + k] * size, size)


def split_rows(index, rows, width, sent, kept):
    half = sent.shape[0]
    core = index[CORE_AT]
    for ref, place in ((sent, 1 - core), (kept, core)):
        ref[:, :width] = low(rows[row_slice(place * half, half), :])


def project_kernel(
    index, h0, h2, h1, h3, query, pair, downs, query_raise, side_raise, sent, kept, q, lo
):
    blocks = (h0, h1, h2, h3)
    size = h0.shape[1]
    cuts = [part_rows(index, k, size) for k in range(4)]
    low_rows = sum(product(blocks[k][...], downs[:, cuts[k]], 1, 1) for k in range(4))
    lo[...] = low_rows
    low_rows = low(low_rows)
    key_value = sum(product(blocks[k][...], pair[:, cuts[k]], 1, 1) for k in range(4))
    key_value = low(key_value + ADAPTER_SCALE * matrix_product(low_rows, side_raise[...]))
    q[...] = ADAPTER_SCALE * matrix_product(low_rows, query_raise[...]) + sum(
        matrix_product(blocks[k][...], query[cuts[k], :]) for k in range(4)
    )
    half, width = sent.shape[0], q.shape[1]
    split_rows(index, q, width, sent, kept)
    split_rows(index, lo, lo.shape[1], sent.at[:, width + 2 * DH :], kept.at[:, width + 2 * DH :])
    for ref in (sent, kept):
        ref[:, width : width + DH] = key_value[:half]
        ref[:, width + DH : width + 2 * DH] = key_value[half:]


def project_back_kernel(
    index, g0, g2, g1, g3, output, output_raise, output_down, sent, kept, g, lo
):
    blocks = (g0, g1, g2, g3)
    size = g0.shape[1]
    cuts = [part_rows(index, k, size) for k in range(4)]
    low_rows = ADAPTER_SCALE * sum(
        product(blocks[k][...], output_raise[:, cuts[k]], 1, 1) for k in range(4)
    )
    lo[...] = low_rows[:, DH:]
    g[...] = matrix_product(low(low_rows), output_down[...]) + sum(
        product(blocks[k][...], output[:, cuts[k]], 1, 1) for k in range(4)
    )
    width = g.shape[1]
    split_rows(index, g, width, sent, kept)
    split_rows(index, lo, DH, sent.at[:, width:], kept.at[:, width:])


def cells_kernel(fold, index, kept, got, c0, c1, c2, c3, total):
    total[...] = wide(kept[...]) + wide(got[...])
    mine = c0.shape[0]
    first, last = fold
    for k, cell in enumerate((c0, c1, c2, c3)):
        rows = row_slice(index[X_BLOCK + k] * mine, mine)
        cell[:, :first] = low(total[rows, :first])
        size = last - first
        for j in range(4 if size else 0):
            cell[:, first + j * size : first + (j + 1) * size] = low(
                total[j * mine : (j + 1) * mine, first:last]
            )
        cell[:, first + 4 * size :] = low(total[rows, last:])


def attend_kernel(
    index,
    own_ref,
    second_ref,
    first_ref,
    third_ref,
    own_side,
    other_side,
    cosine_ref,
    sine_ref,
    cosine_mine_ref,
    sine_mine_ref,
    allowed_ref,
    message_ref,
    probs_ref,
    query_ref,
    key_ref,
    value_ref,
):
    refs = (own_ref, first_ref, second_ref, third_ref)
    mine = cosine_mine_ref.shape[0]
    tokens = cosine_ref.shape[0]
    heads = query_ref.shape[0] // mine
    width = heads * DH
    chunks = tokens // mine

    def total(start, size):
        return tree_sum([ref[:, start : start + size] for ref in refs])

    in_front = lax.broadcasted_iota(jnp.int32, (mine, DH), 1) < HALF
    pair_upper = jnp.full((mine, DH), index[PAIR_AT], jnp.int32) > 0
    for chunk in range(chunks):
        row = (chunk % 2) * (tokens // 2) + (chunk // 2) * mine
        own = wide(own_side[:, chunk * DH : (chunk + 1) * DH])
        other = wide(other_side[:, chunk * DH : (chunk + 1) * DH])
        lower = jnp.where(pair_upper, other, own)
        upper = jnp.where(pair_upper, own, other)
        keys = jnp.where(in_front, lower, pltpu.roll(upper, HALF, 1))
        values = jnp.where(in_front, pltpu.roll(lower, HALF, 1), upper)
        rows = slice(row, row + mine)
        turned = keys * cosine_ref[rows, :] + pltpu.roll(keys, HALF, 1) * sine_ref[rows, :]
        key_ref[rows, :] = low(turned)
        value_ref[rows, :] = low(values)
    cosine, sine = cosine_mine_ref[...], sine_mine_ref[...]
    for head in range(heads):
        queries = total(head * DH, DH)
        turned = queries * cosine + pltpu.roll(queries, HALF, 1) * sine
        query_ref[head * mine : (head + 1) * mine, :] = low(turned)
    scores = product(query_ref[...], key_ref[...], 1, 1) * DH ** (-0.5)
    allowed = jnp.concatenate([allowed_ref[...]] * heads, axis=0) > 0.0
    scores = jnp.where(allowed, scores, -1e30)
    weights = jnp.exp(scores - jnp.max(scores, axis=-1, keepdims=True))
    probs = weights / jnp.sum(weights, axis=-1, keepdims=True)
    probs_ref[...] = probs
    mixed = low(matrix_product(low(probs), value_ref[...]))
    for head in range(heads):
        message_ref[:, head * DH : (head + 1) * DH] = mixed[head * mine : (head + 1) * mine]
    tail = width + DH * chunks
    message_ref[:, width:] = low(total(tail, own_ref.shape[1] - tail))


def attend_back_kernel(
    index,
    own_ref,
    second_ref,
    first_ref,
    third_ref,
    probs_ref,
    query_ref,
    key_ref,
    value_ref,
    cosine_ref,
    sine_ref,
    cosine_mine_ref,
    sine_mine_ref,
    message_ref,
    side_kept,
    side_sent,
    grad_ref,
):
    refs = (own_ref, first_ref, second_ref, third_ref)
    mine = cosine_mine_ref.shape[0]
    tokens = cosine_ref.shape[0]
    heads = query_ref.shape[0] // mine
    width = heads * DH

    def total(start, size):
        return tree_sum([ref[:, start : start + size] for ref in refs])

    for head in range(heads):
        grad_ref[head * mine : (head + 1) * mine, :] = low(total(head * DH, DH))
    grads = grad_ref[...]
    probs = probs_ref[...]
    grad_probs = product(grads, value_ref[...], 1, 1)
    inner = jnp.sum(probs * grad_probs, axis=-1, keepdims=True)
    grad_scores = low(probs * (grad_probs - inner) * DH ** (-0.5))
    keys = product(grad_scores, query_ref[...], 0, 0)
    keys = keys * cosine_ref[...] - pltpu.roll(keys, HALF, 1) * sine_ref[...]
    values = product(low(probs), grads, 0, 0)
    in_front = lax.broadcasted_iota(jnp.int32, (tokens, DH), 1) < HALF
    pair_upper = jnp.full((tokens, DH), index[PAIR_AT], jnp.int32) > 0
    lower = jnp.where(in_front, keys, pltpu.roll(values, HALF, 1))
    upper = jnp.where(in_front, pltpu.roll(keys, HALF, 1), values)
    kept = low(jnp.where(pair_upper, upper, lower))
    sent = low(jnp.where(pair_upper, lower, upper))
    for j in range(tokens // mine):
        side_kept[:, j * DH : (j + 1) * DH] = kept[j * mine : (j + 1) * mine]
        side_sent[:, j * DH : (j + 1) * DH] = sent[j * mine : (j + 1) * mine]
    queries = matrix_product(grad_scores, key_ref[...])
    cosine, sine = cosine_mine_ref[...], sine_mine_ref[...]
    for head in range(heads):
        rows = queries[head * mine : (head + 1) * mine]
        turned = rows * cosine - pltpu.roll(rows, HALF, 1) * sine
        message_ref[:, head * DH : (head + 1) * DH] = low(turned)
    message_ref[:, width:] = low(total(width, own_ref.shape[1] - width))


def join_kernel(index, s0, s2, s1, s3, joined):
    shards = (s0, s1, s2, s3)
    mine = s0.shape[0]
    width = s0.shape[1] - 8 * DH
    for k, shard in enumerate(shards):
        rows = slice(k * mine, (k + 1) * mine)
        joined[rows, :width] = shard[:, :width]
        for half in range(2):
            start = width + (k + 4 * half) * DH
            joined[rows, width + half * DH : width + (half + 1) * DH] = low(
                tree_sum([each[:, start : start + DH] for each in shards])
            )


def place_rows(index, own, got, target):
    half = own.shape[0]
    mine = half // 4
    core = index[CORE_AT]
    for source, place in ((own, core), (got, 1 - core)):
        for k in range(4):
            start = place * half + index[X_BLOCK + k] * mine
            target[row_slice(start, mine), :] = source[k * mine : (k + 1) * mine, :]


def input_kernel(
    index,
    own,
    got,
    query,
    pair,
    downs,
    query_raise,
    side_raise,
    output_down,
    p0,
    p1,
    p2,
    p3,
    low_cell,
    rows_low,
    out_low,
    grads,
    key_value,
    low_sums,
):
    width = query.shape[1]
    size = p0.shape[1]
    tokens = key_value.shape[0]
    half = tokens // 2
    first, last = rows_low.shape[1], own.shape[1] - 2 * DH
    place_rows(index, own.at[:, :first], got.at[:, :first], rows_low)
    place_rows(index, own.at[:, first:last], got.at[:, first:last], grads)
    side = low(wide(own[:, last:]) + wide(got[:, last:]))
    key_value[:half] = side[:, :DH]
    key_value[half:] = side[:, DH:]
    out_low[...] = low(product(rows_low[:, :width], output_down[...], 1, 1))
    raised = product(grads[:, :width], query_raise[...], 1, 1) + product(
        key_value[...], side_raise[...], 1, 1
    )
    low_sums[...] = low(ADAPTER_SCALE * raised + wide(out_low[...]))
    cut = tokens // 4
    for k, ref in enumerate((p0, p1, p2, p3)):
        rows = part_rows(index, k, size)
        part = (
            product(grads[:, :width], query[rows, :], 1, 1)
            + matrix_product(key_value[...], pair[:, rows])
            + matrix_product(low_sums[...], downs[:, rows])
        )
        ref[:tokens, :] = part.astype(ref.dtype)
        low_rows = low_sums[row_slice(index[Y_BLOCK + k] * cut, cut), :]
        target = ref.at[tokens:, :] if k else low_cell
        lows = low_rows.shape[1]
        target[:, :lows] = low_rows[: cut // 2]
        target[:, lows:] = low_rows[cut // 2 :]


def layer_kernel(
    index,
    rows_low,
    out_low,
    grads,
    key_value,
    output,
    output_raise,
    p0,
    p1,
    p2,
    p3,
    width_part,
):
    width = output.shape[0]
    size = p0.shape[1]
    for k, ref in enumerate((p0, p1, p2, p3)):
        columns = part_rows(index, k, size)
        part = matrix_product(
            rows_low[:, :width], output[:, columns]
        ) + ADAPTER_SCALE * matrix_product(out_low[...], output_raise[:, columns])
        ref[...] = part.astype(ref.dtype)
    by_query = ADAPTER_SCALE * product(rows_low[:, width:], grads[:, :width], 0, 0)
    by_side = ADAPTER_SCALE * product(rows_low[:, width:], key_value[...], 0, 0)
    by_output = product(grads[:, width:], rows_low[:, :width], 0, 0)
    rank = DH // 2
    width_part[:rank, :width] = low(by_query[:rank])
    width_part[rank:, :width] = low(by_output[rank:])
    width_part[:, width:] = low(by_side[rank : 3 * rank])


def narrow_kernel(index, own, low_own, g2, g1, g3, c0, c1, c2, c3, low_mine, total):
    tokens, size = c0.shape
    total[...] = (own[...] + wide(g1[:tokens, :])) + (
        wide(g2[:tokens, :]) + wide(g3[:tokens, :])
    )
    if low_own is not None:
        sums = low(
            tree_sum([low_own[...], g1[tokens:, :], g2[tokens:, :], g3[tokens:, :]])
        )
        cut = sums.shape[0]
        for k in range(4):
            low_mine[k * cut : (k + 1) * cut, :] = sums[:, k * size : (k + 1) * size]
    for k, ref in enumerate((c0, c1, c2, c3)):
        cell = total[:, row_slice(index[ZH_BLOCK + k] * size, size)]
        ref[:tokens, :] = cell.astype(ref.dtype)
        if low_own is not None and k:
            ref[tokens:, :] = low_mine[...]


def plain_narrow_kernel(index, own, g2, g1, g3, c0, c1, c2, c3, total):
    narrow_kernel(index, own, None, g2, g1, g3, c0, c1, c2, c3, None, total)


def down_kernel(index, *refs):
    hidden, gradient, other = refs[:4], refs[4:8], refs[8:12]
    low_rows, other_low = refs[12:14]
    outs = refs[14:18]
    rank = outs[0].shape[0]
    tokens, size = hidden[0].shape
    own_left = low(wide(low_rows[...]).T)
    other_left = low(wide(other_low[...]).T)
    cut = 3 * rank
    for k in range(4):
        columns = row_slice(index[Y_BLOCK + k] * size, size)
        down = matrix_product(own_left[:cut], hidden[k][...]) + matrix_product(
            other_left[:cut], other[k][:tokens, :]
        )
        raised = ADAPTER_SCALE * (
            matrix_product(own_left[cut:], gradient[k][...])
            + matrix_product(other_left[cut:], other[k][tokens:, :])
        )
        for j in range(3):
            outs[j][:, columns] = down[j * rank : (j + 1) * rank]
        outs[3][:, columns] = raised


def per_device(
    hidden_input,
    doc_ids,
    cotangent,
    query_matrix,
    key_matrix,
    value_matrix,
    output_matrix,
    query_down,
    query_raise_map,
    key_down,
    key_raise_map,
    value_down,
    value_raise_map,
    output_down,
    output_raise_map,
):
    row_index = lax.axis_index("row")
    col_index = lax.axis_index("col")
    x_index, core_index = row_index >> 1, row_index & 1
    y_index, zh_index = col_index >> 2, col_index & 3
    index = jnp.stack(
        [y_index ^ k for k in range(4)]
        + [zh_index ^ k for k in range(4)]
        + [x_index ^ k for k in range(4)]
        + [core_index, col_index & 1]
    ).astype(jnp.int32)
    tokens, sub_width = hidden_input.shape
    half = tokens // 2
    rank = query_down.shape[0]
    depth, width = query_matrix.shape
    mine = tokens // lax.axis_size("row")
    first = core_index * half + x_index * mine
    quarter = depth // 4
    heads_rows = width // DH * mine
    shape = jax.ShapeDtypeStruct
    short, full = jnp.bfloat16, jnp.float32

    hidden_z = spread(hidden_input, "col", 1)
    gradient_z = spread(cotangent, "col", 1)
    hidden_zh = jnp.concatenate(in_order(hidden_z, zh_index), axis=1)
    hidden_y = spread(hidden_zh, "col", 4)
    gradient_zh = jnp.concatenate(in_order(gradient_z, zh_index), axis=1)
    gradient_y = spread(gradient_zh, "col", 4)
    both = swapped(jnp.concatenate([hidden_zh, gradient_zh], axis=0), "dp", 1)

    (
        doc_row,
        key_matrix,
        value_matrix,
        query_down,
        query_raise_map,
        key_down,
        key_raise_map,
        value_down,
        value_raise_map,
        output_down,
        output_raise_map,
        _,
    ) = lax.optimization_barrier(
        (
            doc_ids[0],
            key_matrix,
            value_matrix,
            query_down,
            query_raise_map,
            key_down,
            key_raise_map,
            value_down,
            value_raise_map,
            output_down,
            output_raise_map,
            hidden_zh,
        )
    )
    cosine, sine = rope_tables(doc_row)
    tables = (
        cosine,
        sine,
        lax.dynamic_slice_in_dim(cosine, first, mine, 0),
        lax.dynamic_slice_in_dim(sine, first, mine, 0),
    )
    places = jnp.arange(tokens, dtype=jnp.int32)
    my_docs = lax.dynamic_slice_in_dim(doc_row, first, mine)
    my_places = first + jnp.arange(mine, dtype=jnp.int32)
    allowed = wide(
        (places[None, :] <= my_places[:, None]) & (doc_row[None, :] == my_docs[:, None])
    )
    pair_matrix = jnp.concatenate([key_matrix.T, value_matrix.T], axis=0)

    def zeros(rows, columns):
        return jnp.zeros((rows, columns), short)

    downs = jnp.concatenate([query_down, key_down, value_down, zeros(rank, depth)], axis=0)
    query_raise = jnp.concatenate([query_raise_map, zeros(3 * rank, width)], axis=0)
    nothing = zeros(rank, rank)
    side_raise = jnp.concatenate(
        [
            zeros(rank, 2 * rank),
            jnp.concatenate([key_raise_map, nothing], axis=1),
            jnp.concatenate([nothing, value_raise_map], axis=1),
            zeros(rank, 2 * rank),
        ],
        axis=0,
    )
    output_down_low = jnp.concatenate([zeros(3 * rank, width), output_down], axis=0)
    output_raise = jnp.concatenate([zeros(3 * rank, depth), output_raise_map], axis=0)
    lows = 4 * rank

    columns = width + 2 * DH + lows
    sent, kept = kernel_call(
        project_kernel,
        (shape((half, columns), short),) * 2,
        (index, *far_first(hidden_y), query_matrix, pair_matrix, downs, query_raise, side_raise),
        scratch=[pltpu.VMEM((tokens, width), full), pltpu.VMEM((tokens, lows), full)],
        flops=2 * tokens * depth * columns,
        name="project",
    )
    columns = width + 8 * DH + lows
    kept, both = lax.optimization_barrier((kept, both))
    other_y = spread(both, "col", 4)
    cells = kernel_call(
        functools.partial(cells_kernel, (width, width + 2 * DH)),
        (shape((mine, columns), short),) * 4,
        (index, kept, swapped(sent, "row", CORE)),
        scratch=[pltpu.VMEM(sent.shape, full)],
        name="cells",
    )
    cells = [cells[0]] + exchanged(cells, "row", 2)
    gradient_y[0], cells[0] = lax.optimization_barrier((gradient_y[0], cells[0]))
    back_sent, back_kept = kernel_call(
        project_back_kernel,
        (shape((half, width + DH), short),) * 2,
        (index, *far_first(gradient_y), output_matrix, output_raise, output_down_low),
        scratch=[pltpu.VMEM((tokens, width), full), pltpu.VMEM((tokens, DH), full)],
        flops=2 * tokens * depth * width,
        name="project_back",
    )
    side = low(tree_sum([cell[:, width : width + 8 * DH] for cell in cells]))
    message, *saved = kernel_call(
        attend_kernel,
        (
            shape((mine, width + lows), short),
            shape((heads_rows, tokens), full),
            shape((heads_rows, DH), short),
            shape((tokens, DH), short),
            shape((tokens, DH), short),
        ),
        (index, *far_first(cells), side, swapped(side, "col", PAIR), *tables, allowed),
        flops=4 * heads_rows * tokens * DH,
        name="attend",
    )
    cells = kernel_call(
        functools.partial(cells_kernel, (width, width)),
        (shape((mine, width + DH), short),) * 4,
        (index, back_kept, swapped(back_sent, "row", CORE)),
        scratch=[pltpu.VMEM(back_sent.shape, full)],
        name="cells_back",
    )
    cells = [cells[0]] + exchanged(cells, "row", 2)
    attention = message
    cells[0], other_y[1], other_y[3] = lax.optimization_barrier(
        (cells[0], other_y[1], other_y[3])
    )
    message, side_kept, side_sent = kernel_call(
        attend_back_kernel,
        (
            shape((mine, width + DH), short),
            shape((mine, 8 * DH), short),
            shape((mine, 8 * DH), short),
        ),
        (index, *far_first(cells), *saved, *tables),
        scratch=[pltpu.VMEM((heads_rows, DH), short)],
        flops=8 * heads_rows * tokens * DH,
        name="attend_back",
    )
    side = low(wide(side_kept) + wide(swapped(side_sent, "col", PAIR)))
    shards = spread(jnp.concatenate([attention, message, side], axis=1), "row", 2)
    shards[0], other_y[2] = lax.optimization_barrier((shards[0], other_y[2]))
    joined = kernel_call(
        join_kernel,
        shape((half, 2 * width + lows + 3 * DH), short),
        (index, *far_first(shards)),
        name="join",
    )
    *parts, low_cell, rows_low, out_low, grads, key_value = kernel_call(
        input_kernel,
        (
            shape((tokens, quarter), full),
            *[shape((tokens + tokens // 8, quarter), short)] * 3,
            shape((tokens // 8, quarter), short),
            shape((tokens, width + lows), short),
            shape((tokens, lows), short),
            shape((tokens, width + DH), short),
            shape((tokens, DH), short),
        ),
        (
            index,
            joined,
            swapped(joined, "row", CORE),
            query_matrix,
            pair_matrix,
            downs,
            query_raise,
            side_raise,
            output_down_low,
        ),
        scratch=[pltpu.VMEM((tokens, lows), short)],
        flops=2 * tokens * depth * width,
        name="input",
    )
    got_input = exchanged(parts, "col", 4)
    rows_low, got_input[0] = lax.optimization_barrier((rows_low, got_input[0]))
    *layer_parts, width_part = kernel_call(
        layer_kernel,
        (
            shape((tokens, quarter), full),
            *[shape((tokens, quarter), short)] * 3,
            shape((2 * rank, width + DH), short),
        ),
        (index, rows_low, out_low, grads, key_value, output_matrix, output_raise),
        flops=2 * tokens * depth * width,
        name="layer",
    )
    got_layer = exchanged(layer_parts, "col", 4)
    width_total = sum_replicas(width_part)
    low_cell, width_part = lax.optimization_barrier((low_cell, width_part))
    *cells, low_mine = kernel_call(
        narrow_kernel,
        (
            shape((tokens, sub_width), full),
            *[shape((tokens + half, sub_width), short)] * 3,
            shape((half, sub_width), short),
        ),
        (index, parts[0], low_cell, *far_first(got_input)),
        scratch=[pltpu.VMEM((tokens, quarter), full)],
        name="narrow_input",
    )
    got = exchanged(cells, "col", 1)
    low_mine = folded(low(tree_sum([low_mine] + [part[tokens:] for part in got])), 4)
    low_mine, layer_parts[0], *got_layer = lax.optimization_barrier(
        (low_mine, layer_parts[0], *got_layer)
    )
    low_rows = jnp.concatenate(
        [unfolded(rows, 2) for rows in in_order(spread(low_mine, "col", 4), y_index)], axis=0
    )
    layer_cells = kernel_call(
        plain_narrow_kernel,
        (shape((tokens, sub_width), full), *[shape((tokens, sub_width), short)] * 3),
        (index, layer_parts[0], *far_first(got_layer)),
        scratch=[pltpu.VMEM((tokens, quarter), full)],
        name="narrow_layer",
    )
    got_layer = exchanged(layer_cells, "col", 1)
    input_grad = (cells[0] + wide(got[0][:tokens])) + (
        wide(got[1][:tokens]) + wide(got[2][:tokens])
    )
    layer_output = (layer_cells[0] + wide(got_layer[0])) + (
        wide(got_layer[1]) + wide(got_layer[2])
    )

    downs_total = kernel_call(
        down_kernel,
        (shape((rank, depth), full),) * 4,
        (index, *hidden_y, *gradient_y, *other_y, low_rows, swapped(low_rows, "dp", 1)),
        flops=4 * tokens * depth * lows,
        name="down_grads",
    )
    return (
        layer_output,
        input_grad,
        downs_total[0],
        width_total[:rank, :width],
        downs_total[1],
        width_total[:rank, width : width + rank],
        downs_total[2],
        width_total[rank:, width + rank :],
        width_total[rank:, :width],
        downs_total[3],
    )


def solution(mesh):
    in_specs = (
        P("dp", ("row", "col")),
        P("dp", None),
        P("dp", ("row", "col")),
        P("row", "col"),
        P("row", "col"),
        P("row", "col"),
        P("col", "row"),
        P(None, "row"),
        P(None, "col"),
        P(None, "row"),
        P(None, "col"),
        P(None, "row"),
        P(None, "col"),
        P(None, "col"),
        P(None, "row"),
    )
    out_specs = (
        P("dp", ("row", "col")),
        P("dp", ("row", "col")),
        P(None, "row"),
        P(None, "col"),
        P(None, "row"),
        P(None, "col"),
        P(None, "row"),
        P(None, "col"),
        P(None, "col"),
        P(None, "row"),
    )
    return jax.shard_map(
        per_device, mesh=mesh, in_specs=in_specs, out_specs=out_specs, check_vma=False
    )
```

```python
import functools

import jax
import jax.numpy as jnp
from jax import lax
from jax.experimental import pallas as pl
from jax.experimental.pallas import tpu as pltpu
from jax.sharding import PartitionSpec as P

DH = 128
HALF = DH // 2
ADAPTER_SCALE = 0.5
ROPE_BASE = 500000.0
CORE = 1
PAIR = 1


def swapped(shard, axis, mask):
    return lax.ppermute(shard, axis, [(i, i ^ mask) for i in range(lax.axis_size(axis))])


def low(rows):
    return rows.astype(jnp.bfloat16)


def wide(rows):
    return rows.astype(jnp.float32)


def matrix_product(left_side, right_side):
    return jnp.dot(left_side, right_side, preferred_element_type=jnp.float32)


def product(left_side, right_side, left_dim, right_dim):
    return lax.dot_general(
        left_side,
        right_side,
        (((left_dim,), (right_dim,)), ((), ())),
        preferred_element_type=jnp.float32,
    )


def spread(shard, axis, unit):
    return [shard] + exchanged([shard] * 4, axis, unit)


def exchanged(shards, axis, unit):
    got = {k: swapped(shards[k], axis, k * unit) for k in (2, 1, 3)}
    return [got[k] for k in (1, 2, 3)]


def in_order(shards, place):
    odd, upper = place & 1 == 1, place >> 1 & 1 == 1
    shards = [jnp.where(odd, shards[j ^ 1], shards[j]) for j in range(4)]
    return [jnp.where(upper, shards[j ^ 2], shards[j]) for j in range(4)]


def tree_sum(shards):
    return (wide(shards[0]) + wide(shards[1])) + (wide(shards[2]) + wide(shards[3]))


def block(array, index, size, dim):
    return lax.dynamic_slice_in_dim(array, index * size, size, dim)


def two_halves(upper, own, other):
    return jnp.where(upper, other, own), jnp.where(upper, own, other)


def folded(rows, parts):
    return jnp.concatenate(jnp.split(rows, parts, axis=0), axis=1)


def unfolded(rows, parts):
    return jnp.concatenate(jnp.split(rows, parts, axis=1), axis=0)


def sum_replicas(part):
    part = low(part)
    return wide(part) + wide(swapped(part, "dp", 1))


def rope_tables(doc_row):
    length = doc_row.shape[0]
    places = jnp.arange(length, dtype=jnp.int32)
    same_doc = doc_row[:, None] == doc_row[None, :]
    doc_start = jnp.min(jnp.where(same_doc, places[None, :], length), axis=1)
    offsets = (places - doc_start).astype(jnp.float32)
    inverse = ROPE_BASE ** (-(jnp.arange(HALF, dtype=jnp.float32) * 2.0 / DH))
    angles = offsets[:, None] * inverse[None, :]
    cosine, sine = jnp.cos(angles), jnp.sin(angles)
    return (
        jnp.concatenate([cosine, cosine], axis=1),
        jnp.concatenate([-sine, sine], axis=1),
    )


def row_slice(start, size):
    return pl.ds(pl.multiple_of(start, size), size)


def far_first(shards):
    return [*shards[:-3], shards[-2], shards[-3], shards[-1]]


def kernel_call(kernel, out_shape, operands, scratch=(), flops=0, name=None, streamed=()):
    vmem = pl.BlockSpec(memory_space=pltpu.VMEM)
    hbm = pl.BlockSpec(memory_space=pltpu.HBM)
    smem = pl.BlockSpec(memory_space=pltpu.SMEM)
    return pl.pallas_call(
        kernel,
        out_shape=out_shape,
        in_specs=[smem] + [hbm if i in streamed else vmem for i in range(1, len(operands))],
        out_specs=jax.tree.map(lambda _: vmem, out_shape),
        scratch_shapes=list(scratch),
        compiler_params=pltpu.CompilerParams(vmem_limit_bytes=15 << 20),
        cost_estimate=pl.CostEstimate(
            flops=flops, bytes_accessed=2 << 20, transcendentals=0
        ),
        name=name,
    )(*operands)


def fetch(source_of, target, arrived):
    copies = [
        pltpu.make_async_copy(source_of(k), target.at[k], arrived.at[k]) for k in range(4)
    ]
    for copy in copies:
        copy.start()
    return copies


Y_BLOCK, ZH_BLOCK, X_BLOCK, CORE_AT, PAIR_AT = 0, 4, 8, 12, 13


def part_rows(index, k, size):
    return row_slice(index[Y_BLOCK + k] * size, size)


def split_rows(index, rows, width, sent, kept):
    half = sent.shape[0]
    core = index[CORE_AT]
    for ref, place in ((sent, 1 - core), (kept, core)):
        ref[:, :width] = low(rows[row_slice(place * half, half), :])


def project_kernel(
    index, h0, h2, h1, h3, query, pair, downs, query_raise, side_raise, sent, kept, q, lo, held, arrived
):
    blocks = (h0, h1, h2, h3)
    size = h0.shape[1]
    cuts = [part_rows(index, k, size) for k in range(4)]
    copies = fetch(lambda k: query.at[cuts[k], :], held, arrived)
    low_rows = sum(product(blocks[k][...], downs[:, cuts[k]], 1, 1) for k in range(4))
    lo[...] = low_rows
    low_rows = low(low_rows)
    key_value = sum(product(blocks[k][...], pair[:, cuts[k]], 1, 1) for k in range(4))
    key_value = low(key_value + ADAPTER_SCALE * matrix_product(low_rows, side_raise[...]))
    for copy in copies:
        copy.wait()
    q[...] = ADAPTER_SCALE * matrix_product(low_rows, query_raise[...]) + sum(
        matrix_product(blocks[k][...], held[k]) for k in range(4)
    )
    half, width = sent.shape[0], q.shape[1]
    split_rows(index, q, width, sent, kept)
    split_rows(index, lo, lo.shape[1], sent.at[:, width + 2 * DH :], kept.at[:, width + 2 * DH :])
    for ref in (sent, kept):
        ref[:, width : width + DH] = key_value[:half]
        ref[:, width + DH : width + 2 * DH] = key_value[half:]


def project_back_kernel(
    index, g0, g2, g1, g3, output, output_raise, output_down, sent, kept, g, lo, held, arrived
):
    blocks = (g0, g1, g2, g3)
    size = g0.shape[1]
    cuts = [part_rows(index, k, size) for k in range(4)]
    copies = fetch(lambda k: output.at[:, cuts[k]], held, arrived)
    low_rows = ADAPTER_SCALE * sum(
        product(blocks[k][...], output_raise[:, cuts[k]], 1, 1) for k in range(4)
    )
    lo[...] = low_rows[:, DH:]
    for copy in copies:
        copy.wait()
    g[...] = matrix_product(low(low_rows), output_down[...]) + sum(
        product(blocks[k][...], held[k], 1, 1) for k in range(4)
    )
    width = g.shape[1]
    split_rows(index, g, width, sent, kept)
    split_rows(index, lo, DH, sent.at[:, width:], kept.at[:, width:])


def cells_kernel(fold, index, kept, got, c0, c1, c2, c3, total):
    total[...] = wide(kept[...]) + wide(got[...])
    mine = c0.shape[0]
    first, last = fold
    for k, cell in enumerate((c0, c1, c2, c3)):
        rows = row_slice(index[X_BLOCK + k] * mine, mine)
        cell[:, :first] = low(total[rows, :first])
        size = last - first
        for j in range(4 if size else 0):
            cell[:, first + j * size : first + (j + 1) * size] = low(
                total[j * mine : (j + 1) * mine, first:last]
            )
        cell[:, first + 4 * size :] = low(total[rows, last:])


def attend_kernel(
    index,
    own_ref,
    second_ref,
    first_ref,
    third_ref,
    own_side,
    other_side,
    cosine_ref,
    sine_ref,
    cosine_mine_ref,
    sine_mine_ref,
    allowed_ref,
    message_ref,
    probs_ref,
    query_ref,
    key_ref,
    value_ref,
):
    refs = (own_ref, first_ref, second_ref, third_ref)
    mine = cosine_mine_ref.shape[0]
    tokens = cosine_ref.shape[0]
    heads = query_ref.shape[0] // mine
    width = heads * DH
    chunks = tokens // mine

    def total(start, size):
        return tree_sum([ref[:, start : start + size] for ref in refs])

    in_front = lax.broadcasted_iota(jnp.int32, (mine, DH), 1) < HALF
    pair_upper = jnp.full((mine, DH), index[PAIR_AT], jnp.int32) > 0
    for chunk in range(chunks):
        row = (chunk % 2) * (tokens // 2) + (chunk // 2) * mine
        own = wide(own_side[:, chunk * DH : (chunk + 1) * DH])
        other = wide(other_side[:, chunk * DH : (chunk + 1) * DH])
        lower = jnp.where(pair_upper, other, own)
        upper = jnp.where(pair_upper, own, other)
        keys = jnp.where(in_front, lower, pltpu.roll(upper, HALF, 1))
        values = jnp.where(in_front, pltpu.roll(lower, HALF, 1), upper)
        rows = slice(row, row + mine)
        turned = keys * cosine_ref[rows, :] + pltpu.roll(keys, HALF, 1) * sine_ref[rows, :]
        key_ref[rows, :] = low(turned)
        value_ref[rows, :] = low(values)
    cosine, sine = cosine_mine_ref[...], sine_mine_ref[...]
    for head in range(heads):
        queries = total(head * DH, DH)
        turned = queries * cosine + pltpu.roll(queries, HALF, 1) * sine
        query_ref[head * mine : (head + 1) * mine, :] = low(turned)
    scores = product(query_ref[...], key_ref[...], 1, 1) * DH ** (-0.5)
    allowed = jnp.concatenate([allowed_ref[...]] * heads, axis=0) > 0.0
    scores = jnp.where(allowed, scores, -1e30)
    weights = jnp.exp(scores - jnp.max(scores, axis=-1, keepdims=True))
    probs = weights / jnp.sum(weights, axis=-1, keepdims=True)
    probs_ref[...] = probs
    mixed = low(matrix_product(low(probs), value_ref[...]))
    for head in range(heads):
        message_ref[:, head * DH : (head + 1) * DH] = mixed[head * mine : (head + 1) * mine]
    tail = width + DH * chunks
    message_ref[:, width:] = low(total(tail, own_ref.shape[1] - tail))


def attend_back_kernel(
    index,
    own_ref,
    second_ref,
    first_ref,
    third_ref,
    probs_ref,
    query_ref,
    key_ref,
    value_ref,
    cosine_ref,
    sine_ref,
    cosine_mine_ref,
    sine_mine_ref,
    message_ref,
    side_kept,
    side_sent,
    grad_ref,
):
    refs = (own_ref, first_ref, second_ref, third_ref)
    mine = cosine_mine_ref.shape[0]
    tokens = cosine_ref.shape[0]
    heads = query_ref.shape[0] // mine
    width = heads * DH

    def total(start, size):
        return tree_sum([ref[:, start : start + size] for ref in refs])

    for head in range(heads):
        grad_ref[head * mine : (head + 1) * mine, :] = low(total(head * DH, DH))
    grads = grad_ref[...]
    probs = probs_ref[...]
    grad_probs = product(grads, value_ref[...], 1, 1)
    inner = jnp.sum(probs * grad_probs, axis=-1, keepdims=True)
    grad_scores = low(probs * (grad_probs - inner) * DH ** (-0.5))
    keys = product(grad_scores, query_ref[...], 0, 0)
    keys = keys * cosine_ref[...] - pltpu.roll(keys, HALF, 1) * sine_ref[...]
    values = product(low(probs), grads, 0, 0)
    in_front = lax.broadcasted_iota(jnp.int32, (tokens, DH), 1) < HALF
    pair_upper = jnp.full((tokens, DH), index[PAIR_AT], jnp.int32) > 0
    lower = jnp.where(in_front, keys, pltpu.roll(values, HALF, 1))
    upper = jnp.where(in_front, pltpu.roll(keys, HALF, 1), values)
    kept = low(jnp.where(pair_upper, upper, lower))
    sent = low(jnp.where(pair_upper, lower, upper))
    for j in range(tokens // mine):
        side_kept[:, j * DH : (j + 1) * DH] = kept[j * mine : (j + 1) * mine]
        side_sent[:, j * DH : (j + 1) * DH] = sent[j * mine : (j + 1) * mine]
    queries = matrix_product(grad_scores, key_ref[...])
    cosine, sine = cosine_mine_ref[...], sine_mine_ref[...]
    for head in range(heads):
        rows = queries[head * mine : (head + 1) * mine]
        turned = rows * cosine - pltpu.roll(rows, HALF, 1) * sine
        message_ref[:, head * DH : (head + 1) * DH] = low(turned)
    message_ref[:, width:] = low(total(width, own_ref.shape[1] - width))


def join_kernel(index, s0, s2, s1, s3, joined):
    shards = (s0, s1, s2, s3)
    mine = s0.shape[0]
    width = s0.shape[1] - 8 * DH
    for k, shard in enumerate(shards):
        rows = slice(k * mine, (k + 1) * mine)
        joined[rows, :width] = shard[:, :width]
        for half in range(2):
            start = width + (k + 4 * half) * DH
            joined[rows, width + half * DH : width + (half + 1) * DH] = low(
                tree_sum([each[:, start : start + DH] for each in shards])
            )


def place_rows(index, own, got, target):
    half = own.shape[0]
    mine = half // 4
    core = index[CORE_AT]
    for source, place in ((own, core), (got, 1 - core)):
        for k in range(4):
            start = place * half + index[X_BLOCK + k] * mine
            target[row_slice(start, mine), :] = source[k * mine : (k + 1) * mine, :]


def input_kernel(
    index,
    own,
    got,
    query,
    pair,
    downs,
    query_raise,
    side_raise,
    output_down,
    p0,
    p1,
    p2,
    p3,
    low_cell,
    rows_low,
    out_low,
    grads,
    key_value,
    low_sums,
):
    width = query.shape[1]
    size = p0.shape[1]
    tokens = key_value.shape[0]
    half = tokens // 2
    first, last = rows_low.shape[1], own.shape[1] - 2 * DH
    place_rows(index, own.at[:, :first], got.at[:, :first], rows_low)
    place_rows(index, own.at[:, first:last], got.at[:, first:last], grads)
    side = low(wide(own[:, last:]) + wide(got[:, last:]))
    key_value[:half] = side[:, :DH]
    key_value[half:] = side[:, DH:]
    out_low[...] = low(product(rows_low[:, :width], output_down[...], 1, 1))
    raised = product(grads[:, :width], query_raise[...], 1, 1) + product(
        key_value[...], side_raise[...], 1, 1
    )
    low_sums[...] = low(ADAPTER_SCALE * raised + wide(out_low[...]))
    cut = tokens // 4
    for k, ref in enumerate((p0, p1, p2, p3)):
        rows = part_rows(index, k, size)
        part = (
            product(grads[:, :width], query[rows, :], 1, 1)
            + matrix_product(key_value[...], pair[:, rows])
            + matrix_product(low_sums[...], downs[:, rows])
        )
        ref[:tokens, :] = part.astype(ref.dtype)
        low_rows = low_sums[row_slice(index[Y_BLOCK + k] * cut, cut), :]
        target = ref.at[tokens:, :] if k else low_cell
        lows = low_rows.shape[1]
        target[:, :lows] = low_rows[: cut // 2]
        target[:, lows:] = low_rows[cut // 2 :]


def layer_kernel(
    index,
    rows_low,
    out_low,
    grads,
    key_value,
    output,
    output_raise,
    p0,
    p1,
    p2,
    p3,
    width_part,
    held,
    arrived,
):
    width = output.shape[0]
    size = p0.shape[1]
    copies = fetch(lambda k: output.at[:, part_rows(index, k, size)], held, arrived)
    for k, ref in enumerate((p0, p1, p2, p3)):
        columns = part_rows(index, k, size)
        copies[k].wait()
        part = matrix_product(
            rows_low[:, :width], held[k]
        ) + ADAPTER_SCALE * matrix_product(out_low[...], output_raise[:, columns])
        ref[...] = part.astype(ref.dtype)
    by_query = ADAPTER_SCALE * product(rows_low[:, width:], grads[:, :width], 0, 0)
    by_side = ADAPTER_SCALE * product(rows_low[:, width:], key_value[...], 0, 0)
    by_output = product(grads[:, width:], rows_low[:, :width], 0, 0)
    rank = DH // 2
    width_part[:rank, :width] = low(by_query[:rank])
    width_part[rank:, :width] = low(by_output[rank:])
    width_part[:, width:] = low(by_side[rank : 3 * rank])


def narrow_kernel(index, own, low_own, g2, g1, g3, c0, c1, c2, c3, low_mine, total):
    tokens, size = c0.shape
    total[...] = (wide(own[...]) + wide(g1[:tokens, :])) + (
        wide(g2[:tokens, :]) + wide(g3[:tokens, :])
    )
    if low_own is not None:
        sums = low(
            tree_sum([low_own[...], g1[tokens:, :], g2[tokens:, :], g3[tokens:, :]])
        )
        cut = sums.shape[0]
        for k in range(4):
            low_mine[k * cut : (k + 1) * cut, :] = sums[:, k * size : (k + 1) * size]
    for k, ref in enumerate((c0, c1, c2, c3)):
        cell = total[:, row_slice(index[ZH_BLOCK + k] * size, size)]
        ref[:tokens, :] = cell.astype(ref.dtype)
        if low_own is not None and k:
            ref[tokens:, :] = low_mine[...]


def plain_narrow_kernel(index, own, g2, g1, g3, c0, c1, c2, c3, total):
    narrow_kernel(index, own, None, g2, g1, g3, c0, c1, c2, c3, None, total)


def down_kernel(index, *refs):
    hidden, gradient, other = refs[:4], refs[4:8], refs[8:12]
    low_rows, other_low = refs[12:14]
    outs = refs[14:18]
    rank = outs[0].shape[0]
    tokens, size = hidden[0].shape
    own_left = low(wide(low_rows[...]).T)
    other_left = low(wide(other_low[...]).T)
    cut = 3 * rank
    for k in range(4):
        columns = row_slice(index[Y_BLOCK + k] * size, size)
        down = matrix_product(own_left[:cut], hidden[k][...]) + matrix_product(
            other_left[:cut], other[k][:tokens, :]
        )
        raised = ADAPTER_SCALE * (
            matrix_product(own_left[cut:], gradient[k][...])
            + matrix_product(other_left[cut:], other[k][tokens:, :])
        )
        for j in range(3):
            outs[j][:, columns] = down[j * rank : (j + 1) * rank]
        outs[3][:, columns] = raised


def per_device(
    hidden_input,
    doc_ids,
    cotangent,
    query_matrix,
    key_matrix,
    value_matrix,
    output_matrix,
    query_down,
    query_raise_map,
    key_down,
    key_raise_map,
    value_down,
    value_raise_map,
    output_down,
    output_raise_map,
):
    row_index = lax.axis_index("row")
    col_index = lax.axis_index("col")
    x_index, core_index = row_index >> 1, row_index & 1
    y_index, zh_index = col_index >> 2, col_index & 3
    index = jnp.stack(
        [y_index ^ k for k in range(4)]
        + [zh_index ^ k for k in range(4)]
        + [x_index ^ k for k in range(4)]
        + [core_index, col_index & 1]
    ).astype(jnp.int32)
    tokens, sub_width = hidden_input.shape
    half = tokens // 2
    rank = query_down.shape[0]
    depth, width = query_matrix.shape
    mine = tokens // lax.axis_size("row")
    first = core_index * half + x_index * mine
    quarter = depth // 4
    heads_rows = width // DH * mine
    shape = jax.ShapeDtypeStruct
    short, full = jnp.bfloat16, jnp.float32

    hidden_z = spread(hidden_input, "col", 1)
    gradient_z = spread(cotangent, "col", 1)
    hidden_zh = jnp.concatenate(in_order(hidden_z, zh_index), axis=1)
    hidden_y = spread(hidden_zh, "col", 4)
    gradient_zh = jnp.concatenate(in_order(gradient_z, zh_index), axis=1)
    gradient_y = spread(gradient_zh, "col", 4)
    both = swapped(jnp.concatenate([hidden_zh, gradient_zh], axis=0), "dp", 1)

    (
        doc_row,
        key_matrix,
        value_matrix,
        query_down,
        query_raise_map,
        key_down,
        key_raise_map,
        value_down,
        value_raise_map,
        output_down,
        output_raise_map,
        _,
    ) = lax.optimization_barrier(
        (
            doc_ids[0],
            key_matrix,
            value_matrix,
            query_down,
            query_raise_map,
            key_down,
            key_raise_map,
            value_down,
            value_raise_map,
            output_down,
            output_raise_map,
            hidden_zh,
        )
    )
    cosine, sine = rope_tables(doc_row)
    tables = (
        cosine,
        sine,
        lax.dynamic_slice_in_dim(cosine, first, mine, 0),
        lax.dynamic_slice_in_dim(sine, first, mine, 0),
    )
    places = jnp.arange(tokens, dtype=jnp.int32)
    my_docs = lax.dynamic_slice_in_dim(doc_row, first, mine)
    my_places = first + jnp.arange(mine, dtype=jnp.int32)
    allowed = wide(
        (places[None, :] <= my_places[:, None]) & (doc_row[None, :] == my_docs[:, None])
    )
    pair_matrix = jnp.concatenate([key_matrix.T, value_matrix.T], axis=0)

    def zeros(rows, columns):
        return jnp.zeros((rows, columns), short)

    downs = jnp.concatenate([query_down, key_down, value_down, zeros(rank, depth)], axis=0)
    query_raise = jnp.concatenate([query_raise_map, zeros(3 * rank, width)], axis=0)
    nothing = zeros(rank, rank)
    side_raise = jnp.concatenate(
        [
            zeros(rank, 2 * rank),
            jnp.concatenate([key_raise_map, nothing], axis=1),
            jnp.concatenate([nothing, value_raise_map], axis=1),
            zeros(rank, 2 * rank),
        ],
        axis=0,
    )
    output_down_low = jnp.concatenate([zeros(3 * rank, width), output_down], axis=0)
    output_raise = jnp.concatenate([zeros(3 * rank, depth), output_raise_map], axis=0)
    lows = 4 * rank

    columns = width + 2 * DH + lows
    sent, kept = kernel_call(
        project_kernel,
        (shape((half, columns), short),) * 2,
        (index, *far_first(hidden_y), query_matrix, pair_matrix, downs, query_raise, side_raise),
        scratch=[
            pltpu.VMEM((tokens, width), full),
            pltpu.VMEM((tokens, lows), full),
            pltpu.VMEM((4, quarter, width), short),
            pltpu.SemaphoreType.DMA((4,)),
        ],
        flops=2 * tokens * depth * columns,
        name="project",
        streamed=(5,),
    )
    columns = width + 8 * DH + lows
    cells = kernel_call(
        functools.partial(cells_kernel, (width, width + 2 * DH)),
        (shape((mine, columns), short),) * 4,
        (index, kept, swapped(sent, "row", CORE)),
        scratch=[pltpu.VMEM(sent.shape, full)],
        name="cells",
    )
    cells = [cells[0]] + exchanged(cells, "row", 2)
    gradient_y[0], cells[0], both = lax.optimization_barrier((gradient_y[0], cells[0], both))
    other_y = spread(both, "col", 4)
    back_sent, back_kept = kernel_call(
        project_back_kernel,
        (shape((half, width + DH), short),) * 2,
        (index, *far_first(gradient_y), output_matrix, output_raise, output_down_low),
        scratch=[
            pltpu.VMEM((tokens, width), full),
            pltpu.VMEM((tokens, DH), full),
            pltpu.VMEM((4, width, quarter), short),
            pltpu.SemaphoreType.DMA((4,)),
        ],
        flops=2 * tokens * depth * width,
        name="project_back",
        streamed=(5,),
    )
    side = low(tree_sum([cell[:, width : width + 8 * DH] for cell in cells]))
    message, *saved = kernel_call(
        attend_kernel,
        (
            shape((mine, width + lows), short),
            shape((heads_rows, tokens), full),
            shape((heads_rows, DH), short),
            shape((tokens, DH), short),
            shape((tokens, DH), short),
        ),
        (index, *far_first(cells), side, swapped(side, "col", PAIR), *tables, allowed),
        flops=4 * heads_rows * tokens * DH,
        name="attend",
    )
    cells = kernel_call(
        functools.partial(cells_kernel, (width, width)),
        (shape((mine, width + DH), short),) * 4,
        (index, back_kept, swapped(back_sent, "row", CORE)),
        scratch=[pltpu.VMEM(back_sent.shape, full)],
        name="cells_back",
    )
    cells = [cells[0]] + exchanged(cells, "row", 2)
    attention = message
    cells[0], other_y[1], other_y[3] = lax.optimization_barrier(
        (cells[0], other_y[1], other_y[3])
    )
    message, side_kept, side_sent = kernel_call(
        attend_back_kernel,
        (
            shape((mine, width + DH), short),
            shape((mine, 8 * DH), short),
            shape((mine, 8 * DH), short),
        ),
        (index, *far_first(cells), *saved, *tables),
        scratch=[pltpu.VMEM((heads_rows, DH), short)],
        flops=8 * heads_rows * tokens * DH,
        name="attend_back",
    )
    side = low(wide(side_kept) + wide(swapped(side_sent, "col", PAIR)))
    shards = spread(jnp.concatenate([attention, message, side], axis=1), "row", 2)
    shards[0], other_y[2] = lax.optimization_barrier((shards[0], other_y[2]))
    joined = kernel_call(
        join_kernel,
        shape((half, 2 * width + lows + 3 * DH), short),
        (index, *far_first(shards)),
        name="join",
    )
    *parts, low_cell, rows_low, out_low, grads, key_value = kernel_call(
        input_kernel,
        (
            shape((tokens, quarter), short),
            *[shape((tokens + tokens // 8, quarter), short)] * 3,
            shape((tokens // 8, quarter), short),
            shape((tokens, width + lows), short),
            shape((tokens, lows), short),
            shape((tokens, width + DH), short),
            shape((tokens, DH), short),
        ),
        (
            index,
            joined,
            swapped(joined, "row", CORE),
            query_matrix,
            pair_matrix,
            downs,
            query_raise,
            side_raise,
            output_down_low,
        ),
        scratch=[pltpu.VMEM((tokens, lows), short)],
        flops=2 * tokens * depth * width,
        name="input",
    )
    got_input = exchanged(parts, "col", 4)
    rows_low, got_input[0] = lax.optimization_barrier((rows_low, got_input[0]))
    *layer_parts, width_part = kernel_call(
        layer_kernel,
        (
            *[shape((tokens, quarter), short)] * 4,
            shape((2 * rank, width + DH), short),
        ),
        (index, rows_low, out_low, grads, key_value, output_matrix, output_raise),
        scratch=[
            pltpu.VMEM((4, width, quarter), short),
            pltpu.SemaphoreType.DMA((4,)),
        ],
        flops=2 * tokens * depth * width,
        name="layer",
        streamed=(5,),
    )
    got_layer = exchanged(layer_parts, "col", 4)
    width_total = sum_replicas(width_part)
    low_cell, width_part = lax.optimization_barrier((low_cell, width_part))
    *cells, low_mine = kernel_call(
        narrow_kernel,
        (
            shape((tokens, sub_width), full),
            *[shape((tokens + half, sub_width), short)] * 3,
            shape((half, sub_width), short),
        ),
        (index, parts[0], low_cell, *far_first(got_input)),
        scratch=[pltpu.VMEM((tokens, quarter), full)],
        name="narrow_input",
    )
    cells[1], cells[2], cells[3], got_layer[0] = lax.optimization_barrier(
        (cells[1], cells[2], cells[3], got_layer[0])
    )
    got = exchanged(cells, "col", 1)
    low_mine = folded(low(tree_sum([low_mine] + [part[tokens:] for part in got])), 4)
    layer_cells = kernel_call(
        plain_narrow_kernel,
        (shape((tokens, sub_width), full), *[shape((tokens, sub_width), short)] * 3),
        (index, layer_parts[0], *far_first(got_layer)),
        scratch=[pltpu.VMEM((tokens, quarter), full)],
        name="narrow_layer",
    )
    got_layer = exchanged(layer_cells, "col", 1)
    low_mine, got_layer[0] = lax.optimization_barrier((low_mine, got_layer[0]))
    low_rows = jnp.concatenate(
        [unfolded(rows, 2) for rows in in_order(spread(low_mine, "col", 4), y_index)], axis=0
    )
    input_grad = (cells[0] + wide(got[0][:tokens])) + (
        wide(got[1][:tokens]) + wide(got[2][:tokens])
    )
    layer_output = (layer_cells[0] + wide(got_layer[0])) + (
        wide(got_layer[1]) + wide(got_layer[2])
    )

    downs_total = kernel_call(
        down_kernel,
        (shape((rank, depth), full),) * 4,
        (index, *hidden_y, *gradient_y, *other_y, low_rows, swapped(low_rows, "dp", 1)),
        flops=80 * tokens * depth * lows,
        name="down_grads",
    )
    return (
        layer_output,
        input_grad,
        downs_total[0],
        width_total[:rank, :width],
        downs_total[1],
        width_total[:rank, width : width + rank],
        downs_total[2],
        width_total[rank:, width + rank :],
        width_total[rank:, :width],
        downs_total[3],
    )


def solution(mesh):
    in_specs = (
        P("dp", ("row", "col")),
        P("dp", None),
        P("dp", ("row", "col")),
        P("row", "col"),
        P("row", "col"),
        P("row", "col"),
        P("col", "row"),
        P(None, "row"),
        P(None, "col"),
        P(None, "row"),
        P(None, "col"),
        P(None, "row"),
        P(None, "col"),
        P(None, "col"),
        P(None, "row"),
    )
    out_specs = (
        P("dp", ("row", "col")),
        P("dp", ("row", "col")),
        P(None, "row"),
        P(None, "col"),
        P(None, "row"),
        P(None, "col"),
        P(None, "row"),
        P(None, "col"),
        P(None, "col"),
        P(None, "row"),
    )
    return jax.shard_map(
        per_device, mesh=mesh, in_specs=in_specs, out_specs=out_specs, check_vma=False
    )
```

```python
import functools

import jax
import jax.numpy as jnp
from jax import lax
from jax.experimental import pallas as pl
from jax.experimental.pallas import tpu as pltpu
from jax.sharding import PartitionSpec as P

DH = 128
HALF = DH // 2
ADAPTER_SCALE = 0.5
ROPE_BASE = 500000.0
CORE = 1
PAIR = 1


def swapped(shard, axis, mask):
    return lax.ppermute(shard, axis, [(i, i ^ mask) for i in range(lax.axis_size(axis))])


def low(rows):
    return rows.astype(jnp.bfloat16)


def wide(rows):
    return rows.astype(jnp.float32)


def matrix_product(left_side, right_side):
    return jnp.dot(left_side, right_side, preferred_element_type=jnp.float32)


def product(left_side, right_side, left_dim, right_dim):
    return lax.dot_general(
        left_side,
        right_side,
        (((left_dim,), (right_dim,)), ((), ())),
        preferred_element_type=jnp.float32,
    )


def spread(shard, axis, unit):
    return [shard] + exchanged([shard] * 4, axis, unit)


def exchanged(shards, axis, unit):
    got = {k: swapped(shards[k], axis, k * unit) for k in (2, 1, 3)}
    return [got[k] for k in (1, 2, 3)]


def in_order(shards, place):
    odd, upper = place & 1 == 1, place >> 1 & 1 == 1
    shards = [jnp.where(odd, shards[j ^ 1], shards[j]) for j in range(4)]
    return [jnp.where(upper, shards[j ^ 2], shards[j]) for j in range(4)]


def tree_sum(shards):
    return (wide(shards[0]) + wide(shards[1])) + (wide(shards[2]) + wide(shards[3]))


def block(array, index, size, dim):
    return lax.dynamic_slice_in_dim(array, index * size, size, dim)


def two_halves(upper, own, other):
    return jnp.where(upper, other, own), jnp.where(upper, own, other)


def folded(rows, parts):
    return jnp.concatenate(jnp.split(rows, parts, axis=0), axis=1)


def unfolded(rows, parts):
    return jnp.concatenate(jnp.split(rows, parts, axis=1), axis=0)


def rope_tables(doc_row):
    length = doc_row.shape[0]
    places = jnp.arange(length, dtype=jnp.int32)
    same_doc = doc_row[:, None] == doc_row[None, :]
    doc_start = jnp.min(jnp.where(same_doc, places[None, :], length), axis=1)
    offsets = (places - doc_start).astype(jnp.float32)
    inverse = ROPE_BASE ** (-(jnp.arange(HALF, dtype=jnp.float32) * 2.0 / DH))
    angles = offsets[:, None] * inverse[None, :]
    cosine, sine = jnp.cos(angles), jnp.sin(angles)
    return (
        jnp.concatenate([cosine, cosine], axis=1),
        jnp.concatenate([-sine, sine], axis=1),
    )


def row_slice(start, size):
    return pl.ds(pl.multiple_of(start, size), size)


def far_first(shards):
    return [*shards[:-3], shards[-2], shards[-3], shards[-1]]


def kernel_call(kernel, out_shape, operands, scratch=(), flops=0, name=None, streamed=()):
    vmem = pl.BlockSpec(memory_space=pltpu.VMEM)
    hbm = pl.BlockSpec(memory_space=pltpu.HBM)
    smem = pl.BlockSpec(memory_space=pltpu.SMEM)
    return pl.pallas_call(
        kernel,
        out_shape=out_shape,
        in_specs=[smem] + [hbm if i in streamed else vmem for i in range(1, len(operands))],
        out_specs=jax.tree.map(lambda _: vmem, out_shape),
        scratch_shapes=list(scratch),
        compiler_params=pltpu.CompilerParams(vmem_limit_bytes=15 << 20),
        cost_estimate=pl.CostEstimate(
            flops=flops, bytes_accessed=2 << 20, transcendentals=0
        ),
        name=name,
    )(*operands)


def fetch(source_of, target, arrived):
    copies = [
        pltpu.make_async_copy(source_of(k), target.at[k], arrived.at[k]) for k in range(4)
    ]
    for copy in copies:
        copy.start()
    return copies


Y_BLOCK, ZH_BLOCK, X_BLOCK, CORE_AT, PAIR_AT = 0, 4, 8, 12, 13


def part_rows(index, k, size):
    return row_slice(index[Y_BLOCK + k] * size, size)


def split_rows(index, rows, width, sent, kept):
    half = sent.shape[0]
    core = index[CORE_AT]
    for ref, place in ((sent, 1 - core), (kept, core)):
        ref[:, :width] = low(rows[row_slice(place * half, half), :])


def project_kernel(
    index, h0, h2, h1, h3, query, pair, downs, query_raise, side_raise, sent, kept, q, lo
):
    blocks = (h0, h1, h2, h3)
    size = h0.shape[1]
    cuts = [part_rows(index, k, size) for k in range(4)]
    low_rows = sum(product(blocks[k][...], downs[:, cuts[k]], 1, 1) for k in range(4))
    lo[...] = low_rows
    low_rows = low(low_rows)
    key_value = sum(product(blocks[k][...], pair[:, cuts[k]], 1, 1) for k in range(4))
    key_value = low(key_value + ADAPTER_SCALE * matrix_product(low_rows, side_raise[...]))
    q[...] = ADAPTER_SCALE * matrix_product(low_rows, query_raise[...]) + sum(
        matrix_product(blocks[k][...], query[cuts[k], :]) for k in range(4)
    )
    half, width = sent.shape[0], q.shape[1]
    split_rows(index, q, width, sent, kept)
    split_rows(index, lo, lo.shape[1], sent.at[:, width + 2 * DH :], kept.at[:, width + 2 * DH :])
    for ref in (sent, kept):
        ref[:, width : width + DH] = key_value[:half]
        ref[:, width + DH : width + 2 * DH] = key_value[half:]


def project_back_kernel(
    index, g0, g2, g1, g3, output, output_raise, output_down, sent, kept, g, lo
):
    blocks = (g0, g1, g2, g3)
    size = g0.shape[1]
    cuts = [part_rows(index, k, size) for k in range(4)]
    low_rows = ADAPTER_SCALE * sum(
        product(blocks[k][...], output_raise[:, cuts[k]], 1, 1) for k in range(4)
    )
    lo[...] = low_rows[:, DH:]
    g[...] = matrix_product(low(low_rows), output_down[...]) + sum(
        product(blocks[k][...], output[:, cuts[k]], 1, 1) for k in range(4)
    )
    width = g.shape[1]
    split_rows(index, g, width, sent, kept)
    split_rows(index, lo, DH, sent.at[:, width:], kept.at[:, width:])


def cells_kernel(fold, index, kept, got, c0, c1, c2, c3, total):
    total[...] = wide(kept[...]) + wide(got[...])
    mine = c0.shape[0]
    first, last = fold
    for k, cell in enumerate((c0, c1, c2, c3)):
        rows = row_slice(index[X_BLOCK + k] * mine, mine)
        cell[:, :first] = low(total[rows, :first])
        size = last - first
        for j in range(4 if size else 0):
            cell[:, first + j * size : first + (j + 1) * size] = low(
                total[j * mine : (j + 1) * mine, first:last]
            )
        cell[:, first + 4 * size :] = low(total[rows, last:])


def attend_kernel(
    index,
    own_ref,
    second_ref,
    first_ref,
    third_ref,
    own_side,
    other_side,
    cosine_ref,
    sine_ref,
    cosine_mine_ref,
    sine_mine_ref,
    allowed_ref,
    message_ref,
    probs_ref,
    query_ref,
    key_ref,
    value_ref,
):
    refs = (own_ref, first_ref, second_ref, third_ref)
    mine = cosine_mine_ref.shape[0]
    tokens = cosine_ref.shape[0]
    heads = query_ref.shape[0] // mine
    width = heads * DH
    chunks = tokens // mine

    def total(start, size):
        return tree_sum([ref[:, start : start + size] for ref in refs])

    in_front = lax.broadcasted_iota(jnp.int32, (mine, DH), 1) < HALF
    pair_upper = jnp.full((mine, DH), index[PAIR_AT], jnp.int32) > 0
    for chunk in range(chunks):
        row = (chunk % 2) * (tokens // 2) + (chunk // 2) * mine
        own = wide(own_side[:, chunk * DH : (chunk + 1) * DH])
        other = wide(other_side[:, chunk * DH : (chunk + 1) * DH])
        lower = jnp.where(pair_upper, other, own)
        upper = jnp.where(pair_upper, own, other)
        keys = jnp.where(in_front, lower, pltpu.roll(upper, HALF, 1))
        values = jnp.where(in_front, pltpu.roll(lower, HALF, 1), upper)
        rows = slice(row, row + mine)
        turned = keys * cosine_ref[rows, :] + pltpu.roll(keys, HALF, 1) * sine_ref[rows, :]
        key_ref[rows, :] = low(turned)
        value_ref[rows, :] = low(values)
    cosine, sine = cosine_mine_ref[...], sine_mine_ref[...]
    for head in range(heads):
        queries = total(head * DH, DH)
        turned = queries * cosine + pltpu.roll(queries, HALF, 1) * sine
        query_ref[head * mine : (head + 1) * mine, :] = low(turned)
    scores = product(query_ref[...], key_ref[...], 1, 1) * DH ** (-0.5)
    allowed = jnp.concatenate([allowed_ref[...]] * heads, axis=0) > 0.0
    scores = jnp.where(allowed, scores, -1e30)
    weights = jnp.exp(scores - jnp.max(scores, axis=-1, keepdims=True))
    probs = weights / jnp.sum(weights, axis=-1, keepdims=True)
    probs_ref[...] = probs
    mixed = low(matrix_product(low(probs), value_ref[...]))
    for head in range(heads):
        message_ref[:, head * DH : (head + 1) * DH] = mixed[head * mine : (head + 1) * mine]
    tail = width + DH * chunks
    message_ref[:, width:] = low(total(tail, own_ref.shape[1] - tail))


def attend_back_kernel(
    index,
    own_ref,
    second_ref,
    first_ref,
    third_ref,
    probs_ref,
    query_ref,
    key_ref,
    value_ref,
    cosine_ref,
    sine_ref,
    cosine_mine_ref,
    sine_mine_ref,
    message_ref,
    side_kept,
    side_sent,
    grad_ref,
):
    refs = (own_ref, first_ref, second_ref, third_ref)
    mine = cosine_mine_ref.shape[0]
    tokens = cosine_ref.shape[0]
    heads = query_ref.shape[0] // mine
    width = heads * DH

    def total(start, size):
        return tree_sum([ref[:, start : start + size] for ref in refs])

    for head in range(heads):
        grad_ref[head * mine : (head + 1) * mine, :] = low(total(head * DH, DH))
    grads = grad_ref[...]
    probs = probs_ref[...]
    grad_probs = product(grads, value_ref[...], 1, 1)
    inner = jnp.sum(probs * grad_probs, axis=-1, keepdims=True)
    grad_scores = low(probs * (grad_probs - inner) * DH ** (-0.5))
    keys = product(grad_scores, query_ref[...], 0, 0)
    keys = keys * cosine_ref[...] - pltpu.roll(keys, HALF, 1) * sine_ref[...]
    values = product(low(probs), grads, 0, 0)
    in_front = lax.broadcasted_iota(jnp.int32, (tokens, DH), 1) < HALF
    pair_upper = jnp.full((tokens, DH), index[PAIR_AT], jnp.int32) > 0
    lower = jnp.where(in_front, keys, pltpu.roll(values, HALF, 1))
    upper = jnp.where(in_front, pltpu.roll(keys, HALF, 1), values)
    kept = low(jnp.where(pair_upper, upper, lower))
    sent = low(jnp.where(pair_upper, lower, upper))
    for j in range(tokens // mine):
        side_kept[:, j * DH : (j + 1) * DH] = kept[j * mine : (j + 1) * mine]
        side_sent[:, j * DH : (j + 1) * DH] = sent[j * mine : (j + 1) * mine]
    queries = matrix_product(grad_scores, key_ref[...])
    cosine, sine = cosine_mine_ref[...], sine_mine_ref[...]
    for head in range(heads):
        rows = queries[head * mine : (head + 1) * mine]
        turned = rows * cosine - pltpu.roll(rows, HALF, 1) * sine
        message_ref[:, head * DH : (head + 1) * DH] = low(turned)
    message_ref[:, width:] = low(total(width, own_ref.shape[1] - width))


def join_kernel(index, s0, s2, s1, s3, joined):
    shards = (s0, s1, s2, s3)
    mine = s0.shape[0]
    width = s0.shape[1] - 8 * DH
    for k, shard in enumerate(shards):
        rows = slice(k * mine, (k + 1) * mine)
        joined[rows, :width] = shard[:, :width]
        for half in range(2):
            start = width + (k + 4 * half) * DH
            joined[rows, width + half * DH : width + (half + 1) * DH] = low(
                tree_sum([each[:, start : start + DH] for each in shards])
            )


def place_rows(index, own, got, target):
    half = own.shape[0]
    mine = half // 4
    core = index[CORE_AT]
    for source, place in ((own, core), (got, 1 - core)):
        for k in range(4):
            start = place * half + index[X_BLOCK + k] * mine
            target[row_slice(start, mine), :] = source[k * mine : (k + 1) * mine, :]


def input_kernel(
    index,
    own,
    got,
    query,
    pair,
    downs,
    query_raise,
    side_raise,
    output_down,
    p0,
    p1,
    p2,
    p3,
    low_cell,
    rows_low,
    out_low,
    grads,
    key_value,
    low_sums,
):
    width = query.shape[1]
    size = p0.shape[1]
    tokens = key_value.shape[0]
    half = tokens // 2
    first, last = rows_low.shape[1], own.shape[1] - 2 * DH
    place_rows(index, own.at[:, :first], got.at[:, :first], rows_low)
    place_rows(index, own.at[:, first:last], got.at[:, first:last], grads)
    side = low(wide(own[:, last:]) + wide(got[:, last:]))
    key_value[:half] = side[:, :DH]
    key_value[half:] = side[:, DH:]
    out_low[...] = low(product(rows_low[:, :width], output_down[...], 1, 1))
    raised = product(grads[:, :width], query_raise[...], 1, 1) + product(
        key_value[...], side_raise[...], 1, 1
    )
    low_sums[...] = low(ADAPTER_SCALE * raised + wide(out_low[...]))
    cut = tokens // 4
    for k, ref in enumerate((p0, p1, p2, p3)):
        rows = part_rows(index, k, size)
        part = (
            product(grads[:, :width], query[rows, :], 1, 1)
            + matrix_product(key_value[...], pair[:, rows])
            + matrix_product(low_sums[...], downs[:, rows])
        )
        ref[:tokens, :] = part.astype(ref.dtype)
        low_rows = low_sums[row_slice(index[Y_BLOCK + k] * cut, cut), :]
        target = ref.at[tokens:, :] if k else low_cell
        lows = low_rows.shape[1]
        target[:, :lows] = low_rows[: cut // 2]
        target[:, lows:] = low_rows[cut // 2 :]


def layer_kernel(
    index,
    rows_low,
    out_low,
    grads,
    key_value,
    output,
    output_raise,
    p0,
    p1,
    p2,
    p3,
    width_part,
    held,
    arrived,
):
    width = output.shape[0]
    size = p0.shape[1]
    copies = fetch(lambda k: output.at[:, part_rows(index, k, size)], held, arrived)
    for k, ref in enumerate((p0, p1, p2, p3)):
        columns = part_rows(index, k, size)
        copies[k].wait()
        part = matrix_product(
            rows_low[:, :width], held[k]
        ) + ADAPTER_SCALE * matrix_product(out_low[...], output_raise[:, columns])
        ref[...] = part.astype(ref.dtype)
    by_query = ADAPTER_SCALE * product(rows_low[:, width:], grads[:, :width], 0, 0)
    by_side = ADAPTER_SCALE * product(rows_low[:, width:], key_value[...], 0, 0)
    by_output = product(grads[:, width:], rows_low[:, :width], 0, 0)
    rank = DH // 2
    width_part[:rank, :width] = low(by_query[:rank])
    width_part[rank:, :width] = low(by_output[rank:])
    width_part[:, width:] = low(by_side[rank : 3 * rank])


def narrow_kernel(index, own, low_own, g2, g1, g3, c0, c1, c2, c3, low_mine, total):
    tokens, size = c0.shape
    total[...] = (wide(own[...]) + wide(g1[:tokens, :])) + (
        wide(g2[:tokens, :]) + wide(g3[:tokens, :])
    )
    if low_own is not None:
        sums = low(
            tree_sum([low_own[...], g1[tokens:, :], g2[tokens:, :], g3[tokens:, :]])
        )
        cut = sums.shape[0]
        for k in range(4):
            low_mine[k * cut : (k + 1) * cut, :] = sums[:, k * size : (k + 1) * size]
    for k, ref in enumerate((c0, c1, c2, c3)):
        cell = total[:, row_slice(index[ZH_BLOCK + k] * size, size)]
        ref[:tokens, :] = cell.astype(ref.dtype)
        if low_own is not None and k:
            ref[tokens:, :] = low_mine[...]


def plain_narrow_kernel(index, own, g2, g1, g3, c0, c1, c2, c3, total):
    narrow_kernel(index, own, None, g2, g1, g3, c0, c1, c2, c3, None, total)


def down_kernel(index, *refs):
    hidden, gradient, other = refs[:4], refs[4:8], refs[8:12]
    low_rows, other_low = refs[12:14]
    outs = refs[14:18]
    rank = outs[0].shape[0]
    tokens, size = hidden[0].shape
    own_left = low(wide(low_rows[...]).T)
    other_left = low(wide(other_low[...]).T)
    cut = 3 * rank
    for k in range(4):
        columns = row_slice(index[Y_BLOCK + k] * size, size)
        down = matrix_product(own_left[:cut], hidden[k][...]) + matrix_product(
            other_left[:cut], other[k][:tokens, :]
        )
        raised = ADAPTER_SCALE * (
            matrix_product(own_left[cut:], gradient[k][...])
            + matrix_product(other_left[cut:], other[k][tokens:, :])
        )
        for j in range(3):
            outs[j][:, columns] = down[j * rank : (j + 1) * rank]
        outs[3][:, columns] = raised


def per_device(
    hidden_input,
    doc_ids,
    cotangent,
    query_matrix,
    key_matrix,
    value_matrix,
    output_matrix,
    query_down,
    query_raise_map,
    key_down,
    key_raise_map,
    value_down,
    value_raise_map,
    output_down,
    output_raise_map,
):
    row_index = lax.axis_index("row")
    col_index = lax.axis_index("col")
    x_index, core_index = row_index >> 1, row_index & 1
    y_index, zh_index = col_index >> 2, col_index & 3
    index = jnp.stack(
        [y_index ^ k for k in range(4)]
        + [zh_index ^ k for k in range(4)]
        + [x_index ^ k for k in range(4)]
        + [core_index, col_index & 1]
    ).astype(jnp.int32)
    tokens, sub_width = hidden_input.shape
    half = tokens // 2
    rank = query_down.shape[0]
    depth, width = query_matrix.shape
    mine = tokens // lax.axis_size("row")
    first = core_index * half + x_index * mine
    quarter = depth // 4
    heads_rows = width // DH * mine
    shape = jax.ShapeDtypeStruct
    short, full = jnp.bfloat16, jnp.float32

    hidden_z = spread(hidden_input, "col", 1)
    gradient_z = spread(cotangent, "col", 1)
    hidden_zh = jnp.concatenate(in_order(hidden_z, zh_index), axis=1)
    hidden_y = spread(hidden_zh, "col", 4)
    gradient_zh = jnp.concatenate(in_order(gradient_z, zh_index), axis=1)
    gradient_y = spread(gradient_zh, "col", 4)
    both = swapped(jnp.concatenate([hidden_zh, gradient_zh], axis=0), "dp", 1)

    (
        doc_row,
        key_matrix,
        value_matrix,
        query_down,
        query_raise_map,
        key_down,
        key_raise_map,
        value_down,
        value_raise_map,
        output_down,
        output_raise_map,
        _,
    ) = lax.optimization_barrier(
        (
            doc_ids[0],
            key_matrix,
            value_matrix,
            query_down,
            query_raise_map,
            key_down,
            key_raise_map,
            value_down,
            value_raise_map,
            output_down,
            output_raise_map,
            hidden_zh,
        )
    )
    cosine, sine = rope_tables(doc_row)
    tables = (
        cosine,
        sine,
        lax.dynamic_slice_in_dim(cosine, first, mine, 0),
        lax.dynamic_slice_in_dim(sine, first, mine, 0),
    )
    places = jnp.arange(tokens, dtype=jnp.int32)
    my_docs = lax.dynamic_slice_in_dim(doc_row, first, mine)
    my_places = first + jnp.arange(mine, dtype=jnp.int32)
    allowed = wide(
        (places[None, :] <= my_places[:, None]) & (doc_row[None, :] == my_docs[:, None])
    )
    pair_matrix = jnp.concatenate([key_matrix.T, value_matrix.T], axis=0)

    def zeros(rows, columns):
        return jnp.zeros((rows, columns), short)

    downs = jnp.concatenate([query_down, key_down, value_down, zeros(rank, depth)], axis=0)
    query_raise = jnp.concatenate([query_raise_map, zeros(3 * rank, width)], axis=0)
    nothing = zeros(rank, rank)
    side_raise = jnp.concatenate(
        [
            zeros(rank, 2 * rank),
            jnp.concatenate([key_raise_map, nothing], axis=1),
            jnp.concatenate([nothing, value_raise_map], axis=1),
            zeros(rank, 2 * rank),
        ],
        axis=0,
    )
    output_down_low = jnp.concatenate([zeros(3 * rank, width), output_down], axis=0)
    output_raise = jnp.concatenate([zeros(3 * rank, depth), output_raise_map], axis=0)
    lows = 4 * rank

    columns = width + 2 * DH + lows
    sent, kept = kernel_call(
        project_kernel,
        (shape((half, columns), short),) * 2,
        (index, *far_first(hidden_y), query_matrix, pair_matrix, downs, query_raise, side_raise),
        scratch=[
            pltpu.VMEM((tokens, width), full),
            pltpu.VMEM((tokens, lows), full),
        ],
        flops=2 * tokens * depth * columns,
        name="project",
    )
    columns = width + 8 * DH + lows
    cells = kernel_call(
        functools.partial(cells_kernel, (width, width + 2 * DH)),
        (shape((mine, columns), short),) * 4,
        (index, kept, swapped(sent, "row", CORE)),
        scratch=[pltpu.VMEM(sent.shape, full)],
        name="cells",
    )
    cells = [cells[0]] + exchanged(cells, "row", 2)
    gradient_y[0], cells[0], both = lax.optimization_barrier((gradient_y[0], cells[0], both))
    other_y = spread(both, "col", 4)
    back_sent, back_kept = kernel_call(
        project_back_kernel,
        (shape((half, width + DH), short),) * 2,
        (index, *far_first(gradient_y), output_matrix, output_raise, output_down_low),
        scratch=[
            pltpu.VMEM((tokens, width), full),
            pltpu.VMEM((tokens, DH), full),
        ],
        flops=2 * tokens * depth * width,
        name="project_back",
    )
    side = low(tree_sum([cell[:, width : width + 8 * DH] for cell in cells]))
    message, *saved = kernel_call(
        attend_kernel,
        (
            shape((mine, width + lows), short),
            shape((heads_rows, tokens), full),
            shape((heads_rows, DH), short),
            shape((tokens, DH), short),
            shape((tokens, DH), short),
        ),
        (index, *far_first(cells), side, swapped(side, "col", PAIR), *tables, allowed),
        flops=4 * heads_rows * tokens * DH,
        name="attend",
    )
    cells = kernel_call(
        functools.partial(cells_kernel, (width, width)),
        (shape((mine, width + DH), short),) * 4,
        (index, back_kept, swapped(back_sent, "row", CORE)),
        scratch=[pltpu.VMEM(back_sent.shape, full)],
        name="cells_back",
    )
    cells = [cells[0]] + exchanged(cells, "row", 2)
    attention = message
    cells[0], other_y[1], other_y[3] = lax.optimization_barrier(
        (cells[0], other_y[1], other_y[3])
    )
    message, side_kept, side_sent = kernel_call(
        attend_back_kernel,
        (
            shape((mine, width + DH), short),
            shape((mine, 8 * DH), short),
            shape((mine, 8 * DH), short),
        ),
        (index, *far_first(cells), *saved, *tables),
        scratch=[pltpu.VMEM((heads_rows, DH), short)],
        flops=8 * heads_rows * tokens * DH,
        name="attend_back",
    )
    side = low(wide(side_kept) + wide(swapped(side_sent, "col", PAIR)))
    shards = spread(jnp.concatenate([attention, message, side], axis=1), "row", 2)
    shards[0], other_y[2] = lax.optimization_barrier((shards[0], other_y[2]))
    joined = kernel_call(
        join_kernel,
        shape((half, 2 * width + lows + 3 * DH), short),
        (index, *far_first(shards)),
        name="join",
    )
    *parts, low_cell, rows_low, out_low, grads, key_value = kernel_call(
        input_kernel,
        (
            shape((tokens, quarter), short),
            *[shape((tokens + tokens // 8, quarter), short)] * 3,
            shape((tokens // 8, quarter), short),
            shape((tokens, width + lows), short),
            shape((tokens, lows), short),
            shape((tokens, width + DH), short),
            shape((tokens, DH), short),
        ),
        (
            index,
            joined,
            swapped(joined, "row", CORE),
            query_matrix,
            pair_matrix,
            downs,
            query_raise,
            side_raise,
            output_down_low,
        ),
        scratch=[pltpu.VMEM((tokens, lows), short)],
        flops=2 * tokens * depth * width,
        name="input",
    )
    got_input = exchanged(parts, "col", 4)
    rows_low, got_input[0] = lax.optimization_barrier((rows_low, got_input[0]))
    *layer_parts, width_part = kernel_call(
        layer_kernel,
        (
            *[shape((tokens, quarter), short)] * 4,
            shape((2 * rank, width + DH), short),
        ),
        (index, rows_low, out_low, grads, key_value, output_matrix, output_raise),
        scratch=[
            pltpu.VMEM((4, width, quarter), short),
            pltpu.SemaphoreType.DMA((4,)),
        ],
        flops=2 * tokens * depth * width,
        name="layer",
        streamed=(5,),
    )
    got_layer = exchanged(layer_parts, "col", 4)
    got_width = swapped(width_part, "dp", 1)
    low_cell, width_part = lax.optimization_barrier((low_cell, width_part))
    *cells, low_mine = kernel_call(
        narrow_kernel,
        (
            shape((tokens, sub_width), full),
            *[shape((tokens + half, sub_width), short)] * 3,
            shape((half, sub_width), short),
        ),
        (index, parts[0], low_cell, *far_first(got_input)),
        scratch=[pltpu.VMEM((tokens, quarter), full)],
        name="narrow_input",
    )
    cells[1], cells[3], got_layer[0] = lax.optimization_barrier(
        (cells[1], cells[3], got_layer[0])
    )
    got = exchanged(cells, "col", 1)
    low_mine = folded(low(tree_sum([low_mine] + [part[tokens:] for part in got])), 4)
    layer_cells = kernel_call(
        plain_narrow_kernel,
        (shape((tokens, sub_width), full), *[shape((tokens, sub_width), short)] * 3),
        (index, layer_parts[0], *far_first(got_layer)),
        scratch=[pltpu.VMEM((tokens, quarter), full)],
        name="narrow_layer",
    )
    low_mine, *layer_cells = lax.optimization_barrier((low_mine, *layer_cells))
    low_shards = spread(low_mine, "col", 4)
    low_shards[1], own_cell, got_width = lax.optimization_barrier(
        (low_shards[1], cells[0], got_width)
    )
    low_rows = jnp.concatenate(
        [unfolded(rows, 2) for rows in in_order(low_shards, y_index)], axis=0
    )
    low_rows, layer_cells[2] = lax.optimization_barrier((low_rows, layer_cells[2]))
    got_layer = exchanged(layer_cells, "col", 1)
    width_total = wide(width_part) + wide(got_width)
    input_grad = (own_cell + wide(got[0][:tokens])) + (
        wide(got[1][:tokens]) + wide(got[2][:tokens])
    )

    downs_total = kernel_call(
        down_kernel,
        (shape((rank, depth), full),) * 4,
        (index, *hidden_y, *gradient_y, *other_y, low_rows, swapped(low_rows, "dp", 1)),
        flops=80 * tokens * depth * lows,
        name="down_grads",
    )
    got_layer[1], first_total = lax.optimization_barrier((got_layer[1], downs_total[0]))
    layer_output = (layer_cells[0] + wide(got_layer[0])) + (
        wide(got_layer[1]) + wide(got_layer[2])
    )
    return (
        layer_output,
        input_grad,
        first_total,
        width_total[:rank, :width],
        downs_total[1],
        width_total[:rank, width : width + rank],
        downs_total[2],
        width_total[rank:, width + rank :],
        width_total[rank:, :width],
        downs_total[3],
    )


def solution(mesh):
    in_specs = (
        P("dp", ("row", "col")),
        P("dp", None),
        P("dp", ("row", "col")),
        P("row", "col"),
        P("row", "col"),
        P("row", "col"),
        P("col", "row"),
        P(None, "row"),
        P(None, "col"),
        P(None, "row"),
        P(None, "col"),
        P(None, "row"),
        P(None, "col"),
        P(None, "col"),
        P(None, "row"),
    )
    out_specs = (
        P("dp", ("row", "col")),
        P("dp", ("row", "col")),
        P(None, "row"),
        P(None, "col"),
        P(None, "row"),
        P(None, "col"),
        P(None, "row"),
        P(None, "col"),
        P(None, "col"),
        P(None, "row"),
    )
    return jax.shard_map(
        per_device, mesh=mesh, in_specs=in_specs, out_specs=out_specs, check_vma=False
    )
```

```python
import functools

import jax
import jax.numpy as jnp
from jax import lax
from jax.experimental import pallas as pl
from jax.experimental.pallas import tpu as pltpu
from jax.sharding import PartitionSpec as P

DH = 128
HALF = DH // 2
ADAPTER_SCALE = 0.5
ROPE_BASE = 500000.0
CORE = 1
PAIR = 1


def swapped(shard, axis, mask):
    return lax.ppermute(shard, axis, [(i, i ^ mask) for i in range(lax.axis_size(axis))])


def low(rows):
    return rows.astype(jnp.bfloat16)


def wide(rows):
    return rows.astype(jnp.float32)


def matrix_product(left_side, right_side):
    return jnp.dot(left_side, right_side, preferred_element_type=jnp.float32)


def product(left_side, right_side, left_dim, right_dim):
    return lax.dot_general(
        left_side,
        right_side,
        (((left_dim,), (right_dim,)), ((), ())),
        preferred_element_type=jnp.float32,
    )


def spread(shard, axis, unit):
    return [shard] + exchanged([shard] * 4, axis, unit)


def exchanged(shards, axis, unit):
    got = {k: swapped(shards[k], axis, k * unit) for k in (2, 1, 3)}
    return [got[k] for k in (1, 2, 3)]


def in_order(shards, place):
    odd, upper = place & 1 == 1, place >> 1 & 1 == 1
    shards = [jnp.where(odd, shards[j ^ 1], shards[j]) for j in range(4)]
    return [jnp.where(upper, shards[j ^ 2], shards[j]) for j in range(4)]


def tree_sum(shards):
    return (wide(shards[0]) + wide(shards[1])) + (wide(shards[2]) + wide(shards[3]))


def block(array, index, size, dim):
    return lax.dynamic_slice_in_dim(array, index * size, size, dim)


def two_halves(upper, own, other):
    return jnp.where(upper, other, own), jnp.where(upper, own, other)


def folded(rows, parts):
    return jnp.concatenate(jnp.split(rows, parts, axis=0), axis=1)


def unfolded(rows, parts):
    return jnp.concatenate(jnp.split(rows, parts, axis=1), axis=0)


def rope_tables(doc_row):
    length = doc_row.shape[0]
    places = jnp.arange(length, dtype=jnp.int32)
    same_doc = doc_row[:, None] == doc_row[None, :]
    doc_start = jnp.min(jnp.where(same_doc, places[None, :], length), axis=1)
    offsets = (places - doc_start).astype(jnp.float32)
    inverse = ROPE_BASE ** (-(jnp.arange(HALF, dtype=jnp.float32) * 2.0 / DH))
    angles = offsets[:, None] * inverse[None, :]
    cosine, sine = jnp.cos(angles), jnp.sin(angles)
    return (
        jnp.concatenate([cosine, cosine], axis=1),
        jnp.concatenate([-sine, sine], axis=1),
    )


def row_slice(start, size):
    return pl.ds(pl.multiple_of(start, size), size)


def far_first(shards):
    return [*shards[:-3], shards[-2], shards[-3], shards[-1]]


def kernel_call(kernel, out_shape, operands, scratch=(), flops=0, name=None, streamed=()):
    vmem = pl.BlockSpec(memory_space=pltpu.VMEM)
    hbm = pl.BlockSpec(memory_space=pltpu.HBM)
    smem = pl.BlockSpec(memory_space=pltpu.SMEM)
    return pl.pallas_call(
        kernel,
        out_shape=out_shape,
        in_specs=[smem] + [hbm if i in streamed else vmem for i in range(1, len(operands))],
        out_specs=jax.tree.map(lambda _: vmem, out_shape),
        scratch_shapes=list(scratch),
        compiler_params=pltpu.CompilerParams(vmem_limit_bytes=15 << 20),
        cost_estimate=pl.CostEstimate(
            flops=flops, bytes_accessed=2 << 20, transcendentals=0
        ),
        name=name,
    )(*operands)


def fetch(source_of, target, arrived):
    copies = [
        pltpu.make_async_copy(source_of(k), target.at[k], arrived.at[k]) for k in range(4)
    ]
    for copy in copies:
        copy.start()
    return copies


Y_BLOCK, ZH_BLOCK, X_BLOCK, CORE_AT, PAIR_AT = 0, 4, 8, 12, 13


def part_rows(index, k, size):
    return row_slice(index[Y_BLOCK + k] * size, size)


def split_rows(index, rows, width, sent, kept):
    half = sent.shape[0]
    core = index[CORE_AT]
    for ref, place in ((sent, 1 - core), (kept, core)):
        ref[:, :width] = low(rows[row_slice(place * half, half), :])


def project_kernel(
    index, h0, h2, h1, h3, query, pair, downs, query_raise, side_raise, sent, kept, q, lo
):
    blocks = (h0, h1, h2, h3)
    size = h0.shape[1]
    cuts = [part_rows(index, k, size) for k in range(4)]
    low_rows = sum(product(blocks[k][...], downs[:, cuts[k]], 1, 1) for k in range(4))
    lo[...] = low_rows
    low_rows = low(low_rows)
    key_value = sum(product(blocks[k][...], pair[:, cuts[k]], 1, 1) for k in range(4))
    key_value = low(key_value + ADAPTER_SCALE * matrix_product(low_rows, side_raise[...]))
    q[...] = ADAPTER_SCALE * matrix_product(low_rows, query_raise[...]) + sum(
        matrix_product(blocks[k][...], query[cuts[k], :]) for k in range(4)
    )
    half, width = sent.shape[0], q.shape[1]
    split_rows(index, q, width, sent, kept)
    split_rows(index, lo, lo.shape[1], sent.at[:, width + 2 * DH :], kept.at[:, width + 2 * DH :])
    for ref in (sent, kept):
        ref[:, width : width + DH] = key_value[:half]
        ref[:, width + DH : width + 2 * DH] = key_value[half:]


def project_back_kernel(
    index, g0, g2, g1, g3, output, output_raise, output_down, sent, kept, g, lo
):
    blocks = (g0, g1, g2, g3)
    size = g0.shape[1]
    cuts = [part_rows(index, k, size) for k in range(4)]
    low_rows = ADAPTER_SCALE * sum(
        product(blocks[k][...], output_raise[:, cuts[k]], 1, 1) for k in range(4)
    )
    lo[...] = low_rows[:, DH:]
    g[...] = matrix_product(low(low_rows), output_down[...]) + sum(
        product(blocks[k][...], output[:, cuts[k]], 1, 1) for k in range(4)
    )
    width = g.shape[1]
    split_rows(index, g, width, sent, kept)
    split_rows(index, lo, DH, sent.at[:, width:], kept.at[:, width:])


def cells_kernel(fold, index, kept, got, c0, c1, c2, c3, total):
    total[...] = wide(kept[...]) + wide(got[...])
    mine = c0.shape[0]
    first, last = fold
    for k, cell in enumerate((c0, c1, c2, c3)):
        rows = row_slice(index[X_BLOCK + k] * mine, mine)
        cell[:, :first] = low(total[rows, :first])
        size = last - first
        for j in range(4 if size else 0):
            cell[:, first + j * size : first + (j + 1) * size] = low(
                total[j * mine : (j + 1) * mine, first:last]
            )
        cell[:, first + 4 * size :] = low(total[rows, last:])


def attend_kernel(
    index,
    own_ref,
    second_ref,
    first_ref,
    third_ref,
    own_side,
    other_side,
    cosine_ref,
    sine_ref,
    cosine_mine_ref,
    sine_mine_ref,
    allowed_ref,
    message_ref,
    probs_ref,
    query_ref,
    key_ref,
    value_ref,
):
    refs = (own_ref, first_ref, second_ref, third_ref)
    mine = cosine_mine_ref.shape[0]
    tokens = cosine_ref.shape[0]
    heads = query_ref.shape[0] // mine
    width = heads * DH
    chunks = tokens // mine

    def total(start, size):
        return tree_sum([ref[:, start : start + size] for ref in refs])

    in_front = lax.broadcasted_iota(jnp.int32, (mine, DH), 1) < HALF
    pair_upper = jnp.full((mine, DH), index[PAIR_AT], jnp.int32) > 0
    for chunk in range(chunks):
        row = (chunk % 2) * (tokens // 2) + (chunk // 2) * mine
        own = wide(own_side[:, chunk * DH : (chunk + 1) * DH])
        other = wide(other_side[:, chunk * DH : (chunk + 1) * DH])
        lower = jnp.where(pair_upper, other, own)
        upper = jnp.where(pair_upper, own, other)
        keys = jnp.where(in_front, lower, pltpu.roll(upper, HALF, 1))
        values = jnp.where(in_front, pltpu.roll(lower, HALF, 1), upper)
        rows = slice(row, row + mine)
        turned = keys * cosine_ref[rows, :] + pltpu.roll(keys, HALF, 1) * sine_ref[rows, :]
        key_ref[rows, :] = low(turned)
        value_ref[rows, :] = low(values)
    cosine, sine = cosine_mine_ref[...], sine_mine_ref[...]
    for head in range(heads):
        queries = total(head * DH, DH)
        turned = queries * cosine + pltpu.roll(queries, HALF, 1) * sine
        query_ref[head * mine : (head + 1) * mine, :] = low(turned)
    scores = product(query_ref[...], key_ref[...], 1, 1) * DH ** (-0.5)
    allowed = jnp.concatenate([allowed_ref[...]] * heads, axis=0) > 0.0
    scores = jnp.where(allowed, scores, -1e30)
    weights = jnp.exp(scores - jnp.max(scores, axis=-1, keepdims=True))
    probs = weights / jnp.sum(weights, axis=-1, keepdims=True)
    probs_ref[...] = probs
    mixed = low(matrix_product(low(probs), value_ref[...]))
    for head in range(heads):
        message_ref[:, head * DH : (head + 1) * DH] = mixed[head * mine : (head + 1) * mine]
    tail = width + DH * chunks
    message_ref[:, width:] = low(total(tail, own_ref.shape[1] - tail))


def attend_back_kernel(
    index,
    own_ref,
    second_ref,
    first_ref,
    third_ref,
    probs_ref,
    query_ref,
    key_ref,
    value_ref,
    cosine_ref,
    sine_ref,
    cosine_mine_ref,
    sine_mine_ref,
    message_ref,
    side_kept,
    side_sent,
    grad_ref,
):
    refs = (own_ref, first_ref, second_ref, third_ref)
    mine = cosine_mine_ref.shape[0]
    tokens = cosine_ref.shape[0]
    heads = query_ref.shape[0] // mine
    width = heads * DH

    def total(start, size):
        return tree_sum([ref[:, start : start + size] for ref in refs])

    for head in range(heads):
        grad_ref[head * mine : (head + 1) * mine, :] = low(total(head * DH, DH))
    grads = grad_ref[...]
    probs = probs_ref[...]
    grad_probs = product(grads, value_ref[...], 1, 1)
    inner = jnp.sum(probs * grad_probs, axis=-1, keepdims=True)
    grad_scores = low(probs * (grad_probs - inner) * DH ** (-0.5))
    keys = product(grad_scores, query_ref[...], 0, 0)
    keys = keys * cosine_ref[...] - pltpu.roll(keys, HALF, 1) * sine_ref[...]
    values = product(low(probs), grads, 0, 0)
    in_front = lax.broadcasted_iota(jnp.int32, (tokens, DH), 1) < HALF
    pair_upper = jnp.full((tokens, DH), index[PAIR_AT], jnp.int32) > 0
    lower = jnp.where(in_front, keys, pltpu.roll(values, HALF, 1))
    upper = jnp.where(in_front, pltpu.roll(keys, HALF, 1), values)
    kept = low(jnp.where(pair_upper, upper, lower))
    sent = low(jnp.where(pair_upper, lower, upper))
    for j in range(tokens // mine):
        side_kept[:, j * DH : (j + 1) * DH] = kept[j * mine : (j + 1) * mine]
        side_sent[:, j * DH : (j + 1) * DH] = sent[j * mine : (j + 1) * mine]
    queries = matrix_product(grad_scores, key_ref[...])
    cosine, sine = cosine_mine_ref[...], sine_mine_ref[...]
    for head in range(heads):
        rows = queries[head * mine : (head + 1) * mine]
        turned = rows * cosine - pltpu.roll(rows, HALF, 1) * sine
        message_ref[:, head * DH : (head + 1) * DH] = low(turned)
    message_ref[:, width:] = low(total(width, own_ref.shape[1] - width))


def join_kernel(index, s0, s2, s1, s3, joined):
    shards = (s0, s1, s2, s3)
    mine = s0.shape[0]
    width = s0.shape[1] - 8 * DH
    for k, shard in enumerate(shards):
        rows = slice(k * mine, (k + 1) * mine)
        joined[rows, :width] = shard[:, :width]
        for half in range(2):
            start = width + (k + 4 * half) * DH
            joined[rows, width + half * DH : width + (half + 1) * DH] = low(
                tree_sum([each[:, start : start + DH] for each in shards])
            )


def place_rows(index, own, got, target):
    half = own.shape[0]
    mine = half // 4
    core = index[CORE_AT]
    for source, place in ((own, core), (got, 1 - core)):
        for k in range(4):
            start = place * half + index[X_BLOCK + k] * mine
            target[row_slice(start, mine), :] = source[k * mine : (k + 1) * mine, :]


def input_kernel(
    index,
    own,
    got,
    query,
    pair,
    downs,
    query_raise,
    side_raise,
    output_down,
    p0,
    p1,
    p2,
    p3,
    low_cell,
    rows_low,
    out_low,
    grads,
    key_value,
    low_sums,
):
    width = query.shape[1]
    size = p0.shape[1]
    tokens = key_value.shape[0]
    half = tokens // 2
    first, last = rows_low.shape[1], own.shape[1] - 2 * DH
    place_rows(index, own.at[:, :first], got.at[:, :first], rows_low)
    place_rows(index, own.at[:, first:last], got.at[:, first:last], grads)
    side = low(wide(own[:, last:]) + wide(got[:, last:]))
    key_value[:half] = side[:, :DH]
    key_value[half:] = side[:, DH:]
    out_low[...] = low(product(rows_low[:, :width], output_down[...], 1, 1))
    raised = product(grads[:, :width], query_raise[...], 1, 1) + product(
        key_value[...], side_raise[...], 1, 1
    )
    low_sums[...] = low(ADAPTER_SCALE * raised + wide(out_low[...]))
    cut = tokens // 4
    for k, ref in enumerate((p0, p1, p2, p3)):
        rows = part_rows(index, k, size)
        part = (
            product(grads[:, :width], query[rows, :], 1, 1)
            + matrix_product(key_value[...], pair[:, rows])
            + matrix_product(low_sums[...], downs[:, rows])
        )
        ref[:tokens, :] = part.astype(ref.dtype)
        low_rows = low_sums[row_slice(index[Y_BLOCK + k] * cut, cut), :]
        target = ref.at[tokens:, :] if k else low_cell
        lows = low_rows.shape[1]
        target[:, :lows] = low_rows[: cut // 2]
        target[:, lows:] = low_rows[cut // 2 :]


def layer_kernel(
    index,
    rows_low,
    out_low,
    grads,
    key_value,
    output,
    output_raise,
    p0,
    p1,
    p2,
    p3,
    width_part,
    held,
    arrived,
):
    width = output.shape[0]
    size = p0.shape[1]
    copies = fetch(lambda k: output.at[:, part_rows(index, k, size)], held, arrived)
    for k, ref in enumerate((p0, p1, p2, p3)):
        columns = part_rows(index, k, size)
        copies[k].wait()
        part = matrix_product(
            rows_low[:, :width], held[k]
        ) + ADAPTER_SCALE * matrix_product(out_low[...], output_raise[:, columns])
        ref[...] = part.astype(ref.dtype)
    by_query = ADAPTER_SCALE * product(rows_low[:, width:], grads[:, :width], 0, 0)
    by_side = ADAPTER_SCALE * product(rows_low[:, width:], key_value[...], 0, 0)
    by_output = product(rows_low[:, width + DH :], rows_low[:, :width], 0, 0)
    rank = DH // 2
    width_part[:rank, :width] = low(by_query[:rank])
    width_part[rank:, :width] = low(by_output[rank:])
    width_part[:, width:] = low(by_side[rank : 3 * rank])


def narrow_kernel(index, own, low_own, g2, g1, g3, c0, c1, c2, c3, low_mine, total):
    tokens, size = c0.shape
    total[...] = (wide(own[...]) + wide(g1[:tokens, :])) + (
        wide(g2[:tokens, :]) + wide(g3[:tokens, :])
    )
    if low_own is not None:
        sums = low(
            tree_sum([low_own[...], g1[tokens:, :], g2[tokens:, :], g3[tokens:, :]])
        )
        cut = sums.shape[0]
        for k in range(4):
            low_mine[k * cut : (k + 1) * cut, :] = sums[:, k * size : (k + 1) * size]
    for k, ref in enumerate((c0, c1, c2, c3)):
        cell = total[:, row_slice(index[ZH_BLOCK + k] * size, size)]
        ref[:tokens, :] = cell.astype(ref.dtype)
        if low_own is not None and k:
            ref[tokens:, :] = low_mine[...]


def plain_narrow_kernel(index, own, g2, g1, g3, c0, c1, c2, c3, total):
    narrow_kernel(index, own, None, g2, g1, g3, c0, c1, c2, c3, None, total)


def down_kernel(index, *refs):
    hidden, gradient, other = refs[:4], refs[4:8], refs[8:12]
    low_rows, other_low = refs[12:14]
    outs = refs[14:18]
    rank = outs[0].shape[0]
    tokens, size = hidden[0].shape
    own_left = low(wide(low_rows[...]).T)
    other_left = low(wide(other_low[...]).T)
    cut = 3 * rank
    for k in range(4):
        columns = row_slice(index[Y_BLOCK + k] * size, size)
        down = matrix_product(own_left[:cut], hidden[k][...]) + matrix_product(
            other_left[:cut], other[k][:tokens, :]
        )
        raised = ADAPTER_SCALE * (
            matrix_product(own_left[cut:], gradient[k][...])
            + matrix_product(other_left[cut:], other[k][tokens:, :])
        )
        for j in range(3):
            outs[j][:, columns] = down[j * rank : (j + 1) * rank]
        outs[3][:, columns] = raised


def per_device(
    hidden_input,
    doc_ids,
    cotangent,
    query_matrix,
    key_matrix,
    value_matrix,
    output_matrix,
    query_down,
    query_raise_map,
    key_down,
    key_raise_map,
    value_down,
    value_raise_map,
    output_down,
    output_raise_map,
):
    row_index = lax.axis_index("row")
    col_index = lax.axis_index("col")
    x_index, core_index = row_index >> 1, row_index & 1
    y_index, zh_index = col_index >> 2, col_index & 3
    index = jnp.stack(
        [y_index ^ k for k in range(4)]
        + [zh_index ^ k for k in range(4)]
        + [x_index ^ k for k in range(4)]
        + [core_index, col_index & 1]
    ).astype(jnp.int32)
    tokens, sub_width = hidden_input.shape
    half = tokens // 2
    rank = query_down.shape[0]
    depth, width = query_matrix.shape
    mine = tokens // lax.axis_size("row")
    first = core_index * half + x_index * mine
    quarter = depth // 4
    heads_rows = width // DH * mine
    shape = jax.ShapeDtypeStruct
    short, full = jnp.bfloat16, jnp.float32

    hidden_z = spread(hidden_input, "col", 1)
    gradient_z = spread(cotangent, "col", 1)
    hidden_zh = jnp.concatenate(in_order(hidden_z, zh_index), axis=1)
    hidden_y = spread(hidden_zh, "col", 4)
    gradient_zh = jnp.concatenate(in_order(gradient_z, zh_index), axis=1)
    gradient_y = spread(gradient_zh, "col", 4)
    both = swapped(jnp.concatenate([hidden_zh, gradient_zh], axis=0), "dp", 1)

    (
        doc_row,
        key_matrix,
        value_matrix,
        query_down,
        query_raise_map,
        key_down,
        key_raise_map,
        value_down,
        value_raise_map,
        output_down,
        output_raise_map,
        _,
    ) = lax.optimization_barrier(
        (
            doc_ids[0],
            key_matrix,
            value_matrix,
            query_down,
            query_raise_map,
            key_down,
            key_raise_map,
            value_down,
            value_raise_map,
            output_down,
            output_raise_map,
            hidden_zh,
        )
    )
    cosine, sine = rope_tables(doc_row)
    tables = (
        cosine,
        sine,
        lax.dynamic_slice_in_dim(cosine, first, mine, 0),
        lax.dynamic_slice_in_dim(sine, first, mine, 0),
    )
    places = jnp.arange(tokens, dtype=jnp.int32)
    my_docs = lax.dynamic_slice_in_dim(doc_row, first, mine)
    my_places = first + jnp.arange(mine, dtype=jnp.int32)
    allowed = wide(
        (places[None, :] <= my_places[:, None]) & (doc_row[None, :] == my_docs[:, None])
    )
    pair_matrix = jnp.concatenate([key_matrix.T, value_matrix.T], axis=0)

    def zeros(rows, columns):
        return jnp.zeros((rows, columns), short)

    downs = jnp.concatenate([query_down, key_down, value_down, zeros(rank, depth)], axis=0)
    query_raise = jnp.concatenate([query_raise_map, zeros(3 * rank, width)], axis=0)
    nothing = zeros(rank, rank)
    side_raise = jnp.concatenate(
        [
            zeros(rank, 2 * rank),
            jnp.concatenate([key_raise_map, nothing], axis=1),
            jnp.concatenate([nothing, value_raise_map], axis=1),
            zeros(rank, 2 * rank),
        ],
        axis=0,
    )
    output_down_low = jnp.concatenate([zeros(3 * rank, width), output_down], axis=0)
    output_raise = jnp.concatenate([zeros(3 * rank, depth), output_raise_map], axis=0)
    lows = 4 * rank

    columns = width + 2 * DH + lows
    sent, kept = kernel_call(
        project_kernel,
        (shape((half, columns), short),) * 2,
        (index, *far_first(hidden_y), query_matrix, pair_matrix, downs, query_raise, side_raise),
        scratch=[
            pltpu.VMEM((tokens, width), full),
            pltpu.VMEM((tokens, lows), full),
        ],
        flops=2 * tokens * depth * columns,
        name="project",
    )
    columns = width + 8 * DH + lows
    cells = kernel_call(
        functools.partial(cells_kernel, (width, width + 2 * DH)),
        (shape((mine, columns), short),) * 4,
        (index, kept, swapped(sent, "row", CORE)),
        scratch=[pltpu.VMEM(sent.shape, full)],
        name="cells",
    )
    cells = [cells[0]] + exchanged(cells, "row", 2)
    gradient_y[0], cells[0], both = lax.optimization_barrier((gradient_y[0], cells[0], both))
    other_y = spread(both, "col", 4)
    back_sent, back_kept = kernel_call(
        project_back_kernel,
        (shape((half, width + DH), short),) * 2,
        (index, *far_first(gradient_y), output_matrix, output_raise, output_down_low),
        scratch=[
            pltpu.VMEM((tokens, width), full),
            pltpu.VMEM((tokens, DH), full),
        ],
        flops=2 * tokens * depth * width,
        name="project_back",
    )
    side = low(tree_sum([cell[:, width : width + 8 * DH] for cell in cells]))
    message, *saved = kernel_call(
        attend_kernel,
        (
            shape((mine, width + lows), short),
            shape((heads_rows, tokens), full),
            shape((heads_rows, DH), short),
            shape((tokens, DH), short),
            shape((tokens, DH), short),
        ),
        (index, *far_first(cells), side, swapped(side, "col", PAIR), *tables, allowed),
        flops=4 * heads_rows * tokens * DH,
        name="attend",
    )
    cells = kernel_call(
        functools.partial(cells_kernel, (width, width)),
        (shape((mine, width + DH), short),) * 4,
        (index, back_kept, swapped(back_sent, "row", CORE)),
        scratch=[pltpu.VMEM(back_sent.shape, full)],
        name="cells_back",
    )
    cells = [cells[0]] + exchanged(cells, "row", 2)
    attention = message
    cells[0], other_y[1], other_y[3] = lax.optimization_barrier(
        (cells[0], other_y[1], other_y[3])
    )
    message, side_kept, side_sent = kernel_call(
        attend_back_kernel,
        (
            shape((mine, width + DH), short),
            shape((mine, 8 * DH), short),
            shape((mine, 8 * DH), short),
        ),
        (index, *far_first(cells), *saved, *tables),
        scratch=[pltpu.VMEM((heads_rows, DH), short)],
        flops=8 * heads_rows * tokens * DH,
        name="attend_back",
    )
    side = low(wide(side_kept) + wide(swapped(side_sent, "col", PAIR)))
    shared = attention[:, width + DH :] + message[:, width:]
    shards = spread(
        jnp.concatenate(
            [attention[:, : width + DH], shared, message[:, :width], side], axis=1
        ),
        "row",
        2,
    )
    shards[0], other_y[2] = lax.optimization_barrier((shards[0], other_y[2]))
    joined = kernel_call(
        join_kernel,
        shape((half, 2 * width + lows + 2 * DH), short),
        (index, *far_first(shards)),
        name="join",
    )
    *parts, low_cell, rows_low, out_low, grads, key_value = kernel_call(
        input_kernel,
        (
            shape((tokens, quarter), short),
            *[shape((tokens + tokens // 8, quarter), short)] * 3,
            shape((tokens // 8, quarter), short),
            shape((tokens, width + lows), short),
            shape((tokens, lows), short),
            shape((tokens, width), short),
            shape((tokens, DH), short),
        ),
        (
            index,
            joined,
            swapped(joined, "row", CORE),
            query_matrix,
            pair_matrix,
            downs,
            query_raise,
            side_raise,
            output_down_low,
        ),
        scratch=[pltpu.VMEM((tokens, lows), short)],
        flops=2 * tokens * depth * width,
        name="input",
    )
    got_input = exchanged(parts, "col", 4)
    rows_low, got_input[0] = lax.optimization_barrier((rows_low, got_input[0]))
    *layer_parts, width_part = kernel_call(
        layer_kernel,
        (
            *[shape((tokens, quarter), short)] * 4,
            shape((2 * rank, width + DH), short),
        ),
        (index, rows_low, out_low, grads, key_value, output_matrix, output_raise),
        scratch=[
            pltpu.VMEM((4, width, quarter), short),
            pltpu.SemaphoreType.DMA((4,)),
        ],
        flops=2 * tokens * depth * width,
        name="layer",
        streamed=(5,),
    )
    got_layer = exchanged(layer_parts, "col", 4)
    got_width = swapped(width_part, "dp", 1)
    low_cell, width_part = lax.optimization_barrier((low_cell, width_part))
    *cells, low_mine = kernel_call(
        narrow_kernel,
        (
            shape((tokens, sub_width), full),
            *[shape((tokens + half, sub_width), short)] * 3,
            shape((half, sub_width), short),
        ),
        (index, parts[0], low_cell, *far_first(got_input)),
        scratch=[pltpu.VMEM((tokens, quarter), full)],
        name="narrow_input",
    )
    cells[1], cells[3], got_layer[0] = lax.optimization_barrier(
        (cells[1], cells[3], got_layer[0])
    )
    got = exchanged(cells, "col", 1)
    low_mine = folded(low(tree_sum([low_mine] + [part[tokens:] for part in got])), 4)
    layer_cells = kernel_call(
        plain_narrow_kernel,
        (shape((tokens, sub_width), full), *[shape((tokens, sub_width), short)] * 3),
        (index, layer_parts[0], *far_first(got_layer)),
        scratch=[pltpu.VMEM((tokens, quarter), full)],
        name="narrow_layer",
    )
    low_mine, *layer_cells = lax.optimization_barrier((low_mine, *layer_cells))
    low_shards = spread(low_mine, "col", 4)
    low_shards[1], own_cell, got_width = lax.optimization_barrier(
        (low_shards[1], cells[0], got_width)
    )
    low_rows = jnp.concatenate(
        [unfolded(rows, 2) for rows in in_order(low_shards, y_index)], axis=0
    )
    low_rows, layer_cells[2] = lax.optimization_barrier((low_rows, layer_cells[2]))
    got_layer = exchanged(layer_cells, "col", 1)
    width_total = wide(width_part) + wide(got_width)
    input_grad = (own_cell + wide(got[0][:tokens])) + (
        wide(got[1][:tokens]) + wide(got[2][:tokens])
    )

    downs_total = kernel_call(
        down_kernel,
        (shape((rank, depth), full),) * 4,
        (index, *hidden_y, *gradient_y, *other_y, low_rows, swapped(low_rows, "dp", 1)),
        flops=80 * tokens * depth * lows,
        name="down_grads",
    )
    got_layer[1], first_total = lax.optimization_barrier((got_layer[1], downs_total[0]))
    layer_output = (layer_cells[0] + wide(got_layer[0])) + (
        wide(got_layer[1]) + wide(got_layer[2])
    )
    return (
        layer_output,
        input_grad,
        first_total,
        width_total[:rank, :width],
        downs_total[1],
        width_total[:rank, width : width + rank],
        downs_total[2],
        width_total[rank:, width + rank :],
        width_total[rank:, :width],
        downs_total[3],
    )


def solution(mesh):
    in_specs = (
        P("dp", ("row", "col")),
        P("dp", None),
        P("dp", ("row", "col")),
        P("row", "col"),
        P("row", "col"),
        P("row", "col"),
        P("col", "row"),
        P(None, "row"),
        P(None, "col"),
        P(None, "row"),
        P(None, "col"),
        P(None, "row"),
        P(None, "col"),
        P(None, "col"),
        P(None, "row"),
    )
    out_specs = (
        P("dp", ("row", "col")),
        P("dp", ("row", "col")),
        P(None, "row"),
        P(None, "col"),
        P(None, "row"),
        P(None, "col"),
        P(None, "row"),
        P(None, "col"),
        P(None, "col"),
        P(None, "row"),
    )
    return jax.shard_map(
        per_device, mesh=mesh, in_specs=in_specs, out_specs=out_specs, check_vma=False
    )
```
